256 devices in a mesh: virt: 64 (over x, z, core), pair: 4 (over y).
Axes of the slice: x: 4, y: 4, z: 8, core: 2. Of those that a mesh axis runs over, the one named last changes fastest.
Arguments:
- amplitudes: bfloat16 [8, 1024, 2, 1024], P('pair'), may hold values from -6 to 6
- integrals: bfloat16 [2, 512, 8, 65536], P(None, None, None, ('virt', 'pair')), may hold values from -0.125 to 0.125
- virt_counts: int32 [8], replicated, may hold values from 32 to 64, as said below
- pair_counts: int32 [8], replicated, may hold values from 512 to 1024, as said below
- pair_list: int32 [8, 1024, 2], P('pair'), may hold values from 0 to 99
- eps_occ: float32 [100], replicated, may hold values from -2 to -0.3
- eps_virt: float32 [512], replicated, may hold values from 0.3 to 4
Outputs:
- update: bfloat16 [8, 1024, 32768], P('pair', None, 'virt')
- pair_energy: float32 [8, 1024], P('pair', 'virt')
The draws below stay inside these ranges and needn't reach their ends.
Inputs may be any that keep to these rules, and one draw needn't show every extreme that they name: virt_counts[0] = 64; every count is at least 32. `pair_counts`: some pair symmetry has exactly 1024 pairs; every count is at least 512.
All inputs are finite; a program needn't handle non-finite values.
Results may differ from the reference program's by a relative error of at most 0.001.
Values may be sent and summed in bfloat16 or wider, within the bound.
No kernel may reach another device: no remote copies, remote signals or barrier semaphores. Data moves between devices by JAX's collectives and lax.ppermute only.
A program may use at most 128 MiB of HBM per device.

```python
import math
import jax
import jax.numpy as jnp
from jax import lax

IRREPS = 8
NV = 512
NOCC = 100
BLK = 64
CS = 16
SLABS = 2
KS = 1024
PCAP = 1024


def draw_virt_counts(key, part):
    counts = jax.random.randint(key, (IRREPS,), BLK // 2, BLK + 1)
    return counts.at[0].set(BLK).astype(jnp.int32)


def draw_pair_counts(key, part):
    first, second = jax.random.split(jax.random.fold_in(key, 11))
    counts = jax.random.randint(first, (IRREPS,), PCAP // 2, PCAP + 1)
    where_full = jax.random.randint(second, (), 0, IRREPS)
    return counts.at[where_full].set(PCAP).astype(jnp.int32)


def set_ends(entries, stream_key, smallest, largest):
    dims = entries.shape
    index_at = [jax.random.randint(jax.random.fold_in(stream_key, axis), (), 0, dims[axis]) for axis in range(len(dims))]
    entries = entries.at[tuple(index_at)].set(smallest)
    longest = dims.index(max(dims))
    index_at[longest] = (index_at[longest] + 1) % dims[longest]
    return entries.at[tuple(index_at)].set(largest)


def levels(stream_key, dims, cuts, least, largest):
    factor_of = 1.0
    for position, shards_of in cuts:
        heights = jax.random.uniform(jax.random.fold_in(jax.random.fold_in(stream_key, 6), position), (shards_of,), jnp.float32, least / len(cuts), largest / len(cuts))
        factor_of = factor_of * jnp.repeat(jnp.exp(heights), dims[position] // shards_of).reshape((-1,) + (1,) * (len(dims) - 1 - position))
    return factor_of


def centred(rng, extent, deviation, limit, pieces=(), held_as=jnp.bfloat16):
    result = jax.random.normal(rng, extent, jnp.float32) * deviation
    if len(pieces) > 0:
        result = levels(rng, extent, pieces, -0.22, 0.18) * result
    return jnp.clip(result, min=-limit, max=limit).astype(held_as)


def setup_inputs(seed: int = 0) -> dict:
    seeds = jax.random.split(jax.random.key(seed), 8)
    return {
        "amplitudes": centred(seeds[0], (IRREPS, PCAP, SLABS, KS), 1.0, 6.0, ((0, 4),)),
        "integrals": centred(seeds[1], (SLABS, NV, IRREPS, BLK * KS), (KS * SLABS) ** -0.5, 0.125, ((3, 256),)),
        "virt_counts": draw_virt_counts(jax.random.fold_in(seeds[7], 71), 0),
        "pair_counts": draw_pair_counts(jax.random.fold_in(seeds[7], 71), 0),
        "pair_list": set_ends(jax.random.randint(seeds[4], (IRREPS, PCAP, 2), 0, NOCC), jax.random.fold_in(seeds[4], 1), 0, NOCC - 1).astype(jnp.int32),
        "eps_occ": jnp.clip(jax.random.uniform(seeds[5], (NOCC,), jnp.float32, -2.0, -0.3), -2.0, -0.3),
        "eps_virt": jnp.clip(jnp.exp(jax.random.uniform(seeds[6], (NV,), jnp.float32, math.log(0.3), math.log(4.0))), 0.3, 4.0),
    }


def reference(amplitudes, integrals, virt_counts, pair_counts, pair_list, eps_occ, eps_virt):
    slots = jnp.arange(BLK, dtype=jnp.int32)
    live_virt = slots[None, :] < virt_counts[:, None]
    a_index = jnp.arange(NV, dtype=jnp.int32)
    a_irrep = a_index // BLK
    a_slot = a_index % BLK
    live_a = jnp.take(live_virt.reshape(-1), a_irrep * BLK + a_slot)
    eps_table = eps_virt.reshape(IRREPS, BLK)
    row_index = jnp.arange(PCAP, dtype=jnp.int32)

    def one_irrep(h):
        dmask = jnp.tile(live_virt[h], CS).astype(jnp.bfloat16)
        masked = amplitudes[h] * dmask[None, None, :]
        ladder = jnp.zeros((PCAP, NV * BLK), jnp.float32)
        for s in range(SLABS):
            block = integrals[s][:, h, :].reshape(NV * BLK, KS)
            ladder = ladder + lax.dot_general(masked[:, s, :], block, (((1,), (1,)), ((), ())), preferred_element_type=jnp.float32)
        ladder = ladder.reshape(PCAP, NV, BLK)
        b_irrep = jnp.bitwise_xor(a_irrep, h)
        eps_b = eps_table[b_irrep]
        live_b = live_virt[b_irrep]
        pairs = pair_list[h]
        occ = eps_occ[pairs[:, 0]] + eps_occ[pairs[:, 1]]
        denom = (eps_virt[:, None] + eps_b)[None, :, :] - occ[:, None, None]
        live = (row_index < pair_counts[h])[:, None, None] & live_a[None, :, None] & live_b[None, :, :]
        ratio = jnp.where(live, ladder / denom, jnp.zeros_like(ladder))
        update = ratio.astype(jnp.bfloat16).reshape(PCAP, NV * BLK)
        energy = jnp.sum(ratio * ladder, axis=(1, 2)) / (NV * BLK)
        return update, energy

    updates, energies = lax.map(one_irrep, jnp.arange(IRREPS, dtype=jnp.int32))
    return updates, energies
```

```python
import jax
import jax.numpy as jnp
from jax import lax
from jax.experimental import pallas as pl
from jax.experimental.pallas import tpu as pltpu
from jax.sharding import PartitionSpec as P

IRREPS = 8
NV = 512
BLK = 64
CS = 16
SLABS = 2
PCAP = 1024
KQ = 256
VMEM = 48 * 1024 * 1024
ABLK = 64
RBLK = 256


def regroup_kernel(pair_ref, x_ref, *refs):
    outs, (perm, held) = refs[:10], refs[10:]
    slab = pl.program_id(0)
    rows = ABLK * IRREPS

    @pl.when((slab == 0) & (pl.program_id(1) == 0))
    def _():
        to = lax.broadcasted_iota(jnp.int32, (rows, rows), 0)
        source = lax.broadcasted_iota(jnp.int32, (rows, rows), 1)
        perm[...] = jnp.where((to % ABLK) * IRREPS + to // ABLK == source, 1.0, 0.0).astype(jnp.bfloat16)

    moved = jnp.dot(perm[...], x_ref[0], preferred_element_type=jnp.float32)
    held[...] = moved.astype(jnp.bfloat16).reshape(IRREPS, ABLK, KQ)
    me = pair_ref[0]
    for parity in range(2):
        own, plus, minus, far0, far1 = outs[5 * parity : 5 * parity + 5]
        own[0] = held[2 * me + parity]
        plus[0] = held[2 * ((me + 1) % 4) + parity]
        minus[0] = held[2 * ((me + 3) % 4) + parity]
        far = 2 * ((me + 2) % 4) + parity

        @pl.when(slab == 0)
        def _():
            far0[...] = held[far]

        @pl.when(slab == 1)
        def _():
            far1[...] = held[far]


def regroup(pair_id, integrals):
    blocks = NV // ABLK
    both = jax.ShapeDtypeStruct((SLABS, NV, KQ), jnp.bfloat16)
    one = jax.ShapeDtypeStruct((NV, KQ), jnp.bfloat16)
    both_spec = pl.BlockSpec((1, ABLK, KQ), lambda s, i, me: (s, i, 0))
    far0_spec = pl.BlockSpec((ABLK, KQ), lambda s, i, me: (jnp.where(s == 0, i, blocks - 1), 0))
    far1_spec = pl.BlockSpec((ABLK, KQ), lambda s, i, me: (jnp.where(s == 1, i, 0), 0))
    flat = integrals.reshape(SLABS, NV * IRREPS, KQ)
    return pl.pallas_call(
        regroup_kernel,
        grid_spec=pltpu.PrefetchScalarGridSpec(
            num_scalar_prefetch=1,
            grid=(SLABS, blocks),
            in_specs=[pl.BlockSpec((1, ABLK * IRREPS, KQ), lambda s, i, me: (s, i, 0))],
            out_specs=[both_spec, both_spec, both_spec, far0_spec, far1_spec] * 2,
            scratch_shapes=[
                pltpu.VMEM((ABLK * IRREPS, ABLK * IRREPS), jnp.bfloat16),
                pltpu.VMEM((IRREPS, ABLK, KQ), jnp.bfloat16),
            ],
        ),
        out_shape=[both, both, both, one, one] * 2,
        compiler_params=pltpu.CompilerParams(vmem_limit_bytes=VMEM),
        name="regroup",
    )(pair_id, flat)


def ladder_kernel(pair_ref, own, left, right, far0, far1, amp, cols, rows, send, energy):
    me = pair_ref[0]

    def term(block, slab, source):
        at = pl.multiple_of(source * KQ, KQ)
        return lax.dot_general(
            block,
            amp[slab, :, pl.ds(at, KQ)],
            (((1,), (1,)), ((), ())),
            preferred_element_type=jnp.float32,
        )

    total = None
    for slab in range(SLABS):
        far = far0 if slab == 0 else far1
        for block, shift in ((own[slab], 0), (left[slab], 3), (right[slab], 1), (far[...], 2)):
            piece = term(block, slab, (me + shift) % 4)
            total = piece if total is None else total + piece
    denom = cols[:, 0:1] - rows[0:1, :]
    live = (cols[:, 1:2] * rows[1:2, :]) > 0.5
    ratio = jnp.where(live, total / denom, 0.0)
    send[...] = ratio.astype(jnp.bfloat16)
    energy[...] = jnp.sum(ratio * total, axis=0, keepdims=True) / (NV * BLK)


def ladder(pair_id, pieces, amp, cols, rows):
    whole = lambda *shape: pl.BlockSpec(shape, lambda i, me: (0,) * len(shape))
    return pl.pallas_call(
        ladder_kernel,
        grid_spec=pltpu.PrefetchScalarGridSpec(
            num_scalar_prefetch=1,
            grid=(PCAP // RBLK,),
            in_specs=[
                whole(SLABS, NV, KQ),
                whole(SLABS, NV, KQ),
                whole(SLABS, NV, KQ),
                whole(NV, KQ),
                whole(NV, KQ),
                pl.BlockSpec((SLABS, RBLK, 4 * KQ), lambda i, me: (0, i, 0)),
                whole(NV, 8),
                pl.BlockSpec((8, RBLK), lambda i, me: (0, i)),
            ],
            out_specs=[
                pl.BlockSpec((NV, RBLK), lambda i, me: (0, i)),
                pl.BlockSpec((1, RBLK), lambda i, me: (0, i)),
            ],
        ),
        out_shape=[
            jax.ShapeDtypeStruct((NV, PCAP), jnp.bfloat16),
            jax.ShapeDtypeStruct((1, PCAP), jnp.float32),
        ],
        compiler_params=pltpu.CompilerParams(vmem_limit_bytes=VMEM),
        cost_estimate=pl.CostEstimate(
            flops=2 * NV * PCAP * 2048, bytes_accessed=7 << 20, transcendentals=0
        ),
        name="ladder",
    )(pair_id, *pieces, amp, cols, rows)


def place_kernel(first, second, out, perm):
    @pl.when((pl.program_id(0) == 0) & (pl.program_id(1) == 0))
    def _():
        source = lax.broadcasted_iota(jnp.int32, (NV, NV), 0)
        to = lax.broadcasted_iota(jnp.int32, (NV, NV), 1)
        perm[...] = jnp.where((source % 8) * BLK + source // 8 == to, 1.0, 0.0).astype(jnp.bfloat16)

    def put(block):
        out[0] = lax.dot_general(
            block[...], perm[...], (((0,), (0,)), ((), ())), preferred_element_type=jnp.float32
        ).astype(jnp.bfloat16)

    @pl.when(pl.program_id(0) == 0)
    def _():
        put(first)

    @pl.when(pl.program_id(0) == 1)
    def _():
        put(second)


def place(first, second):
    steps = PCAP // RBLK
    return pl.pallas_call(
        place_kernel,
        grid=(2, steps),
        in_specs=[
            pl.BlockSpec((NV, RBLK), lambda h, i: (0, jnp.where(h == 0, i, steps - 1))),
            pl.BlockSpec((NV, RBLK), lambda h, i: (0, jnp.where(h == 1, i, 0))),
        ],
        out_specs=pl.BlockSpec((1, RBLK, NV), lambda h, i: (h, i, 0)),
        out_shape=jax.ShapeDtypeStruct((2, PCAP, NV), jnp.bfloat16),
        scratch_shapes=[pltpu.VMEM((NV, NV), jnp.bfloat16)],
        compiler_params=pltpu.CompilerParams(vmem_limit_bytes=VMEM),
        name="place",
    )(first, second)


def pick(ids, table):
    onehot = ids[..., None] == jnp.arange(table.shape[0], dtype=jnp.int32)
    return jnp.sum(jnp.where(onehot, table, 0), axis=-1)


def step(value, by):
    return lax.ppermute(value, "pair", [(i, (i + by) % 4) for i in range(4)])


def shards(amplitudes, integrals, virt_counts, pair_counts, pair_list, eps_occ, eps_virt):
    me = lax.axis_index("pair")
    virt = lax.axis_index("virt")
    pair_id = me.astype(jnp.int32)[None]
    irrep_ids = me * 2 + jnp.arange(2, dtype=jnp.int32)

    sends = regroup(pair_id, integrals)

    slots = jnp.arange(BLK, dtype=jnp.int32)
    live_d = slots[None, :] < pick(irrep_ids, virt_counts)[:, None]
    dmask = jnp.tile(live_d, (1, CS)).astype(jnp.bfloat16)

    a_irrep = jnp.arange(NV, dtype=jnp.int32) // BLK
    a_slot = jnp.arange(NV, dtype=jnp.int32) % BLK
    b_irrep = jnp.bitwise_xor(jnp.arange(IRREPS, dtype=jnp.int32)[None, :], irrep_ids[:, None])
    eps_at = lax.dynamic_slice_in_dim(eps_virt.reshape(IRREPS, BLK), virt, 1, axis=1)[:, 0]
    eps_b = jnp.repeat(pick(b_irrep, eps_at), BLK, axis=1)
    live_b = jnp.repeat(virt < pick(b_irrep, virt_counts), BLK, axis=1)
    live_a = a_slot < jnp.repeat(virt_counts, BLK)
    col_eps = eps_virt[None, :] + eps_b
    col_live = (live_a[None, :] & live_b).astype(jnp.float32)
    cols = jnp.pad(jnp.stack([col_eps, col_live], axis=-1), ((0, 0), (0, 0), (0, 6)))
    occ_terms = pick(pair_list, eps_occ)
    occ = occ_terms[:, :, 0] + occ_terms[:, :, 1]
    row_live = (
        jnp.arange(PCAP, dtype=jnp.int32)[None, :] < pick(irrep_ids, pair_counts)[:, None]
    ).astype(jnp.float32)
    rows = jnp.pad(jnp.stack([occ, row_live], axis=1), ((0, 0), (0, 6), (0, 0)))

    def exchange(own, plus, minus, far0, far1):
        far0, far1 = step(far0, 1), step(far1, -1)
        left, right = step(plus, 1), step(minus, -1)
        return own, left, right, step(far0, 1), step(far1, -1)

    def masked(parity):
        return jnp.transpose(amplitudes[parity] * dmask[parity][None, None, :], (1, 0, 2))

    even, odd = sends[:5], sends[5:]
    even = exchange(*even)
    even, odd = lax.optimization_barrier((even, odd))
    odd = exchange(*odd)
    send, energy0 = ladder(pair_id, even, masked(0), cols[0], rows[0])
    first = lax.all_to_all(send, "virt", 0, 0, tiled=True)
    first, odd = lax.optimization_barrier((first, odd))
    send, energy1 = ladder(pair_id, odd, masked(1), cols[1], rows[1])
    second = lax.all_to_all(send, "virt", 0, 0, tiled=True)
    terms = jnp.concatenate([energy0, energy1], axis=0).reshape(2, 64, 16)
    terms = jnp.transpose(terms, (1, 0, 2)).reshape(64, 32)
    terms = lax.all_to_all(terms, "virt", 0, 0, tiled=True)
    energy = jnp.sum(terms, axis=0).reshape(2, 16)
    return place(first, second), energy


def solution(mesh):
    placed = (
        P("pair", None, None, None),
        P(None, None, None, ("virt", "pair")),
        P(),
        P(),
        P("pair", None, None),
        P(),
        P(),
    )
    return jax.shard_map(
        shards,
        mesh=mesh,
        in_specs=placed,
        out_specs=(P("pair", None, "virt"), P("pair", "virt")),
        check_vma=False,
    )
```

```python
import jax
import jax.numpy as jnp
from jax import lax
from jax.experimental import pallas as pl
from jax.experimental.pallas import tpu as pltpu
from jax.sharding import PartitionSpec as P

IRREPS = 8
NV = 512
BLK = 64
SLABS = 2
PCAP = 1024
KQ = 256
KS = 1024
VIRTS = 64
OWN = NV // VIRTS
MINE = PCAP // VIRTS
VMEM = 48 * 1024 * 1024
ABLK = 256
SUB = 32
RBLK = 256
EXTRA = 128


def iota(shape, axis):
    return lax.broadcasted_iota(jnp.int32, shape, axis)


def regroup_kernel(pair_ref, x_ref, even, own, plus, far, minus, perm, held):
    rows = SUB * IRREPS

    @pl.when((pl.program_id(0) == 0) & (pl.program_id(1) == 0))
    def _():
        to, source = iota((rows, rows), 0), iota((rows, rows), 1)
        at = (to & (SUB - 1)) * IRREPS + (to >> 5)
        perm[...] = jnp.where(at == source, 1.0, 0.0).astype(jnp.bfloat16)

    for sub in range(ABLK // SUB):
        block = x_ref[0, sub * rows : (sub + 1) * rows, :]
        moved = jnp.dot(perm[...], block, preferred_element_type=jnp.float32).astype(jnp.bfloat16)
        at = slice(sub * SUB, (sub + 1) * SUB)
        for pair in range(4):
            even[pair, 0, at, :] = moved[(2 * pair) * SUB : (2 * pair + 1) * SUB]
            held[pair, at, :] = moved[(2 * pair + 1) * SUB : (2 * pair + 2) * SUB]
    me = pair_ref[0]
    own[0] = held[me]
    plus[0] = held[(me + 1) % 4]
    far[0] = held[(me + 2) % 4]
    minus[0] = held[(me + 3) % 4]


def regroup(pair_id, integrals):
    each = jax.ShapeDtypeStruct((SLABS, NV, KQ), jnp.bfloat16)
    spec = pl.BlockSpec((1, ABLK, KQ), lambda s, i, me: (s, i, 0))
    return pl.pallas_call(
        regroup_kernel,
        grid_spec=pltpu.PrefetchScalarGridSpec(
            num_scalar_prefetch=1,
            grid=(SLABS, NV // ABLK),
            in_specs=[pl.BlockSpec((1, ABLK * IRREPS, KQ), lambda s, i, me: (s, i, 0))],
            out_specs=[pl.BlockSpec((4, 1, ABLK, KQ), lambda s, i, me: (0, s, i, 0))] + [spec] * 4,
            scratch_shapes=[
                pltpu.VMEM((SUB * IRREPS, SUB * IRREPS), jnp.bfloat16),
                pltpu.VMEM((4, ABLK, KQ), jnp.bfloat16),
            ],
        ),
        out_shape=[jax.ShapeDtypeStruct((4, SLABS, NV, KQ), jnp.bfloat16)] + [each] * 4,
        compiler_params=pltpu.CompilerParams(vmem_limit_bytes=VMEM),
        name="regroup",
    )(pair_id, integrals.reshape(SLABS, NV * IRREPS, KQ))


def ladder_kernel(parity, ids, virt_counts, pair_counts, eps, *refs):
    if parity == 0:
        moved, amp, eps_a, occ, send, energy, held = refs
    else:
        own, left, far, right, amp, eps_a, occ, energy0, send, held, energies = refs
    me, virt = ids[0], ids[1]
    h = 2 * me + parity
    at_row = pl.program_id(0)

    @pl.when(at_row == 0)
    def _():
        mask = jnp.where((iota((1, KQ), 1) & (BLK - 1)) < virt_counts[h], 1.0, 0.0).astype(jnp.bfloat16)
        for slab in range(SLABS):
            if parity == 0:
                for source in range(4):
                    to = slab * KS + source * KQ
                    held[:, to : to + KQ] = moved[source, slab] * mask
            else:
                for shift, piece in ((0, own), (3, left), (2, far), (1, right)):
                    to = pl.multiple_of(slab * KS + ((me + shift) % 4) * KQ, KQ)
                    held[:, pl.ds(to, KQ)] = piece[slab] * mask

    total = None
    for slab in range(SLABS):
        term = lax.dot_general(
            held[:, slab * KS : (slab + 1) * KS],
            amp[slab, 0],
            (((1,), (1,)), ((), ())),
            preferred_element_type=jnp.float32,
        )
        total = term if total is None else total + term
    columns = pl.ds(pl.multiple_of(at_row * RBLK, RBLK), RBLK)
    occ_row = occ[parity : parity + 1, :]
    slot = iota((BLK, RBLK), 0)
    live_row = at_row * RBLK + iota((BLK, RBLK), 1) < pair_counts[h]
    summed = jnp.zeros((1, RBLK), jnp.float32)
    for ha in range(IRREPS):
        hb = jnp.bitwise_xor(h, ha)
        part = total[ha * BLK : (ha + 1) * BLK]
        denom = (eps_a[ha * BLK : (ha + 1) * BLK, :] + eps[hb * BLK + virt]) - occ_row
        live_a = jnp.where(virt < virt_counts[hb], virt_counts[ha], 0)
        ratio = jnp.where((slot < live_a) & live_row, part / denom, 0.0)
        summed = summed + jnp.sum(ratio * part, axis=0, keepdims=True)
        ratio = ratio.astype(jnp.bfloat16)
        if parity == 0:
            send[ha * BLK : (ha + 1) * BLK, :] = ratio
        else:
            send[ha * BLK : (ha + 1) * BLK, columns] = ratio
    summed = summed / (NV * BLK)
    if parity == 0:
        energy[...] = summed
        return
    energies[1:2, columns] = summed

    @pl.when(at_row == PCAP // RBLK - 1)
    def _():
        energies[0:1, :] = energy0[...]
        value = energies[0:2, :]
        high = value.astype(jnp.bfloat16).astype(jnp.float32)
        rest = value - high
        middle = rest.astype(jnp.bfloat16).astype(jnp.float32)
        low = rest - middle
        pieces = jnp.concatenate([high, middle, low, jnp.zeros((2, PCAP), jnp.float32)], axis=0)
        spread = jnp.broadcast_to(pieces[None], (VIRTS, OWN, PCAP)).reshape(NV, PCAP)
        owner = (iota((NV, PCAP), 1) // MINE) == (iota((NV, PCAP), 0) // OWN)
        spread = jnp.where(owner, spread, 0.0).astype(jnp.bfloat16)
        lane = (iota((PCAP, EXTRA), 0) & (MINE - 1)) == iota((PCAP, EXTRA), 1)
        select = jnp.where(lane, 1.0, 0.0).astype(jnp.bfloat16)
        send[:, PCAP : PCAP + EXTRA] = jnp.dot(
            spread, select, preferred_element_type=jnp.float32
        ).astype(jnp.bfloat16)


def ladder(parity, scalars, pieces, amp, eps_a, occ, energy0=None):
    whole = lambda *shape: pl.BlockSpec(shape, lambda i, *_: (0,) * len(shape))
    in_specs = [whole(*piece.shape) for piece in pieces] + [
        pl.BlockSpec((SLABS, 1, RBLK, KS), lambda i, *_: (0, parity, i, 0)),
        whole(NV, 1),
        pl.BlockSpec((2, RBLK), lambda i, *_: (0, i)),
    ]
    args = [*scalars, *pieces, amp, eps_a, occ]
    scratch = [pltpu.VMEM((NV, SLABS * KS), jnp.bfloat16)]
    if parity == 0:
        out_specs = [
            pl.BlockSpec((NV, RBLK), lambda i, *_: (0, i)),
            pl.BlockSpec((1, RBLK), lambda i, *_: (0, i)),
        ]
        out_shape = [
            jax.ShapeDtypeStruct((NV, PCAP), jnp.bfloat16),
            jax.ShapeDtypeStruct((1, PCAP), jnp.float32),
        ]
    else:
        in_specs.append(whole(1, PCAP))
        args.append(energy0)
        out_specs = whole(NV, PCAP + EXTRA)
        out_shape = jax.ShapeDtypeStruct((NV, PCAP + EXTRA), jnp.bfloat16)
        scratch.append(pltpu.VMEM((8, PCAP), jnp.float32))
    return pl.pallas_call(
        lambda *refs: ladder_kernel(parity, *refs),
        grid_spec=pltpu.PrefetchScalarGridSpec(
            num_scalar_prefetch=4,
            grid=(PCAP // RBLK,),
            in_specs=in_specs,
            out_specs=out_specs,
            scratch_shapes=scratch,
        ),
        out_shape=out_shape,
        compiler_params=pltpu.CompilerParams(vmem_limit_bytes=VMEM),
        cost_estimate=pl.CostEstimate(
            flops=2 * NV * PCAP * SLABS * KS, bytes_accessed=7 << 20, transcendentals=0
        ),
        name="ladder",
    )(*args)


def put(block, out, perm):
    @pl.when(pl.program_id(0) == 0)
    def _():
        source, to = iota((NV, NV), 0), iota((NV, NV), 1)
        at = (source & (OWN - 1)) * BLK + (source >> 3)
        perm[...] = jnp.where(at == to, 1.0, 0.0).astype(jnp.bfloat16)

    out[0] = lax.dot_general(
        block[...], perm[...], (((0,), (0,)), ((), ())), preferred_element_type=jnp.float32
    ).astype(jnp.bfloat16)


def place_even_kernel(block, out, perm):
    put(block, out, perm)


def place_odd_kernel(block, extra, before, out, energy, perm):
    put(block, out, perm)

    @pl.when(pl.program_id(0) == 0)
    def _():
        values = extra[...].astype(jnp.float32)
        kind = iota((NV, EXTRA), 0) & (OWN - 1)
        for parity in range(2):
            mine = (kind < 6) & ((kind & 1) == parity)
            summed = jnp.sum(jnp.where(mine, values, 0.0), axis=0, keepdims=True)
            energy[parity : parity + 1, :] = summed[:, :MINE]


def place(parity, block, before=None):
    in_specs = [pl.BlockSpec((NV, RBLK), lambda i: (0, i))]
    out_spec = pl.BlockSpec((1, RBLK, NV), lambda i: (parity, i, 0))
    out = jax.ShapeDtypeStruct((2, PCAP, NV), jnp.bfloat16)
    common = dict(
        grid=(PCAP // RBLK,),
        scratch_shapes=[pltpu.VMEM((NV, NV), jnp.bfloat16)],
        compiler_params=pltpu.CompilerParams(vmem_limit_bytes=VMEM),
        cost_estimate=pl.CostEstimate(flops=2 * NV * NV * PCAP, bytes_accessed=2 << 20, transcendentals=0),
        name="place",
    )
    if parity == 0:
        return pl.pallas_call(place_even_kernel, in_specs=in_specs, out_specs=out_spec, out_shape=out, **common)(block)
    in_specs += [
        pl.BlockSpec((NV, EXTRA), lambda i: (0, PCAP // EXTRA)),
        pl.BlockSpec(memory_space=pl.ANY),
    ]
    return pl.pallas_call(
        place_odd_kernel,
        in_specs=in_specs,
        out_specs=[out_spec, pl.BlockSpec((2, MINE), lambda i: (0, 0))],
        out_shape=[out, jax.ShapeDtypeStruct((2, MINE), jnp.float32)],
        input_output_aliases={2: 0},
        **common,
    )(block, block, before)


def pick(ids, table):
    onehot = ids[..., None] == jnp.arange(table.shape[0], dtype=jnp.int32)
    return jnp.sum(jnp.where(onehot, table, 0), axis=-1)


def step(value, by):
    return lax.ppermute(value, "pair", [(i, (i + by) % 4) for i in range(4)])


def across(value):
    return lax.all_to_all(value, "virt", 0, 0, tiled=True)


def shards(amplitudes, integrals, virt_counts, pair_counts, pair_list, eps_occ, eps_virt):
    me = lax.axis_index("pair").astype(jnp.int32)
    virt = lax.axis_index("virt").astype(jnp.int32)
    even, own, plus, far, minus = regroup(me[None], integrals)
    even = lax.all_to_all(even, "pair", 0, 0, tiled=True)

    amp = jnp.transpose(amplitudes, (2, 0, 1, 3))
    occ_terms = pick(pair_list, eps_occ)
    occ = occ_terms[:, :, 0] + occ_terms[:, :, 1]
    eps_a = eps_virt[:, None]
    scalars = (jnp.stack([me, virt]), virt_counts, pair_counts, eps_virt)

    even, plus, far, minus = lax.optimization_barrier((even, plus, far, minus))
    left, far, right = step(plus, 1), step(far, 2), step(minus, 3)
    send, energy0 = ladder(0, scalars, (even,), amp, eps_a, occ)
    first = across(send)
    send = ladder(1, scalars, (own, left, far, right), amp, eps_a, occ, energy0)
    first, send = lax.optimization_barrier((first, send))
    second = across(send)
    out = place(0, first)
    return tuple(place(1, second, out))


def solution(mesh):
    placed = (
        P("pair", None, None, None),
        P(None, None, None, ("virt", "pair")),
        P(),
        P(),
        P("pair", None, None),
        P(),
        P(),
    )
    return jax.shard_map(
        shards,
        mesh=mesh,
        in_specs=placed,
        out_specs=(P("pair", None, "virt"), P("pair", "virt")),
        check_vma=False,
    )
```

```python
import jax
import jax.numpy as jnp
from jax import lax
from jax.experimental import pallas as pl
from jax.experimental.pallas import tpu as pltpu
from jax.sharding import PartitionSpec as P

IRREPS = 8
NV = 512
BLK = 64
SLABS = 2
PCAP = 1024
KQ = 256
KS = 1024
VIRTS = 64
OWN = NV // VIRTS
MINE = PCAP // VIRTS
VMEM = 20 * 1024 * 1024
ABLK = 256
SUB = 32
RBLK = 256


def iota(shape, axis):
    return lax.broadcasted_iota(jnp.int32, shape, axis)


def regroup_kernel(pair_ref, x_ref, even, own, plus, far, minus, perm, held):
    rows = SUB * IRREPS

    @pl.when((pl.program_id(0) == 0) & (pl.program_id(1) == 0))
    def _():
        to, source = iota((rows, rows), 0), iota((rows, rows), 1)
        at = (to & (SUB - 1)) * IRREPS + (to >> 5)
        perm[...] = jnp.where(at == source, 1.0, 0.0).astype(jnp.bfloat16)

    for sub in range(ABLK // SUB):
        block = x_ref[0, sub * rows : (sub + 1) * rows, :]
        moved = jnp.dot(perm[...], block, preferred_element_type=jnp.float32).astype(jnp.bfloat16)
        at = slice(sub * SUB, (sub + 1) * SUB)
        for pair in range(4):
            even[pair, 0, at, :] = moved[(2 * pair) * SUB : (2 * pair + 1) * SUB]
            held[pair, at, :] = moved[(2 * pair + 1) * SUB : (2 * pair + 2) * SUB]
    me = pair_ref[0]
    own[0] = held[me]
    plus[0] = held[(me + 1) % 4]
    far[0] = held[(me + 2) % 4]
    minus[0] = held[(me + 3) % 4]


def regroup(pair_id, integrals):
    each = pltpu.HBM((SLABS, NV, KQ), jnp.bfloat16)
    spec = pl.BlockSpec((1, ABLK, KQ), lambda s, i, me: (s, i, 0))
    return pl.pallas_call(
        regroup_kernel,
        grid_spec=pltpu.PrefetchScalarGridSpec(
            num_scalar_prefetch=1,
            grid=(SLABS, NV // ABLK),
            in_specs=[pl.BlockSpec((1, ABLK * IRREPS, KQ), lambda s, i, me: (s, i, 0))],
            out_specs=[pl.BlockSpec((4, 1, ABLK, KQ), lambda s, i, me: (0, s, i, 0))] + [spec] * 4,
            scratch_shapes=[
                pltpu.VMEM((SUB * IRREPS, SUB * IRREPS), jnp.bfloat16),
                pltpu.VMEM((4, ABLK, KQ), jnp.bfloat16),
            ],
        ),
        out_shape=[pltpu.HBM((4, SLABS, NV, KQ), jnp.bfloat16)] + [each] * 4,
        compiler_params=pltpu.CompilerParams(vmem_limit_bytes=3 * VMEM),
        name="regroup",
    )(pair_id, integrals.reshape(SLABS, NV * IRREPS, KQ))


def ladder_kernel(parity, ids, virt_counts, pair_counts, eps, *refs):
    pieces, (amp, eps_a, occ, send, energy, held, stage, sems) = refs[:-8], refs[-8:]
    me, virt = ids[0], ids[1]
    h = 2 * me + parity
    mask = jnp.where((iota((1, KQ), 1) & (BLK - 1)) < virt_counts[h], 1.0, 0.0).astype(jnp.bfloat16)
    for slab in range(SLABS):
        if parity == 0:
            for source in range(4):
                to = slab * KS + source * KQ
                held[:, to : to + KQ] = pieces[0][source, slab] * mask
        else:
            for shift, piece in zip((0, 3, 2, 1), pieces):
                to = pl.multiple_of(slab * KS + ((me + shift) % 4) * KQ, KQ)
                held[:, pl.ds(to, KQ)] = piece[slab] * mask
    slot = iota((BLK, RBLK), 0)
    column = iota((BLK, RBLK), 1)
    copies = []
    for block in range(PCAP // RBLK):
        at = slice(block * RBLK, (block + 1) * RBLK)
        total = None
        for slab in range(SLABS):
            term = lax.dot_general(
                held[:, slab * KS : (slab + 1) * KS],
                amp[slab, at, :],
                (((1,), (1,)), ((), ())),
                preferred_element_type=jnp.float32,
            )
            total = term if total is None else total + term
        occ_row = occ[parity : parity + 1, at]
        live_row = block * RBLK + column < pair_counts[h]
        summed = jnp.zeros((1, RBLK), jnp.float32)
        for ha in range(IRREPS):
            rows = slice(ha * BLK, (ha + 1) * BLK)
            hb = jnp.bitwise_xor(h, ha)
            part = total[rows]
            denom = (eps_a[rows, :] + eps[hb * BLK + virt]) - occ_row
            live_a = jnp.where(virt < virt_counts[hb], virt_counts[ha], 0)
            ratio = jnp.where((slot < live_a) & live_row, part / denom, 0.0)
            summed = summed + jnp.sum(ratio * part, axis=0, keepdims=True)
            stage[block, rows, :] = ratio.astype(jnp.bfloat16)
        energy[:, at] = summed / (NV * BLK)
        copy = pltpu.make_async_copy(stage.at[block], send.at[:, pl.ds(block * RBLK, RBLK)], sems.at[block])
        copy.start()
        copies.append(copy)
    for copy in copies:
        copy.wait()


def ladder(parity, scalars, pieces, amp, eps_a, occ):
    vmem = pl.BlockSpec(memory_space=pltpu.VMEM)
    return pl.pallas_call(
        lambda *refs: ladder_kernel(parity, *refs),
        in_specs=[pl.BlockSpec(memory_space=pltpu.SMEM)] * 4 + [vmem] * (len(pieces) + 3),
        out_specs=[pl.BlockSpec(memory_space=pl.ANY), vmem],
        out_shape=[
            jax.ShapeDtypeStruct((NV, PCAP), jnp.bfloat16),
            jax.ShapeDtypeStruct((1, PCAP), jnp.float32),
        ],
        scratch_shapes=[
            pltpu.VMEM((NV, SLABS * KS), jnp.bfloat16),
            pltpu.VMEM((PCAP // RBLK, NV, RBLK), jnp.bfloat16),
            pltpu.SemaphoreType.DMA((PCAP // RBLK,)),
        ],
        compiler_params=pltpu.CompilerParams(vmem_limit_bytes=VMEM),
        cost_estimate=pl.CostEstimate(
            flops=2 * NV * PCAP * SLABS * KS, bytes_accessed=7 << 20, transcendentals=0
        ),
        name="ladder",
    )(*scalars, *pieces, amp, eps_a, occ)


def put(block, out, perm):
    @pl.when(pl.program_id(0) == 0)
    def _():
        source, to = iota((NV, NV), 0), iota((NV, NV), 1)
        at = (source & (OWN - 1)) * BLK + (source >> 3)
        perm[...] = jnp.where(at == to, 1.0, 0.0).astype(jnp.bfloat16)

    out[0] = lax.dot_general(
        block[...], perm[...], (((0,), (0,)), ((), ())), preferred_element_type=jnp.float32
    ).astype(jnp.bfloat16)


def place_even_kernel(block, out, perm):
    put(block, out, perm)


def place_odd_kernel(block, before, out, perm):
    put(block, out, perm)


def place(parity, block, before=None):
    in_specs = [pl.BlockSpec((NV, RBLK), lambda i: (0, i))]
    common = dict(
        grid=(PCAP // RBLK,),
        out_specs=pl.BlockSpec((1, RBLK, NV), lambda i: (parity, i, 0)),
        out_shape=jax.ShapeDtypeStruct((2, PCAP, NV), jnp.bfloat16),
        scratch_shapes=[pltpu.VMEM((NV, NV), jnp.bfloat16)],
        compiler_params=pltpu.CompilerParams(vmem_limit_bytes=VMEM),
        cost_estimate=pl.CostEstimate(flops=2 * NV * NV * PCAP, bytes_accessed=2 << 20, transcendentals=0),
        name="place",
    )
    if parity == 0:
        return pl.pallas_call(place_even_kernel, in_specs=in_specs, **common)(block)
    in_specs.append(pl.BlockSpec(memory_space=pl.ANY))
    return pl.pallas_call(
        place_odd_kernel, in_specs=in_specs, input_output_aliases={1: 0}, **common
    )(block, before)


def pick(ids, table):
    onehot = ids[..., None] == jnp.arange(table.shape[0], dtype=jnp.int32)
    return jnp.sum(jnp.where(onehot, table, 0), axis=-1)


def step(value, by):
    return lax.ppermute(value, "pair", [(i, (i + by) % 4) for i in range(4)])


def across(value):
    return lax.all_to_all(value, "virt", 0, 0, tiled=True)


def shards(amplitudes, integrals, virt_counts, pair_counts, pair_list, eps_occ, eps_virt):
    me = lax.axis_index("pair").astype(jnp.int32)
    virt = lax.axis_index("virt").astype(jnp.int32)
    even, own, plus, far, minus = regroup(me[None], integrals)
    even = lax.all_to_all(even, "pair", 0, 0, tiled=True)

    amp = [jnp.transpose(amplitudes[parity], (1, 0, 2)) for parity in range(2)]
    occ_terms = pick(pair_list, eps_occ)
    occ = occ_terms[:, :, 0] + occ_terms[:, :, 1]
    eps_a = eps_virt[:, None]
    scalars = (jnp.stack([me, virt]), virt_counts, pair_counts, eps_virt)

    even, plus, far, minus = lax.optimization_barrier((even, plus, far, minus))
    left, far, right = step(plus, 1), step(far, 2), step(minus, 3)
    send, energy0 = ladder(0, scalars, (even,), amp[0], eps_a, occ)
    first = across(send)
    send, energy1 = ladder(1, scalars, (own, left, far, right), amp[1], eps_a, occ)
    first, send = lax.optimization_barrier((first, send))
    second = across(send)
    energy = jnp.concatenate([energy0, energy1], axis=0)
    for bit in range(6):
        energy = energy + lax.ppermute(energy, "virt", [(i, i ^ (1 << bit)) for i in range(VIRTS)])
    energy = lax.dynamic_slice_in_dim(energy, virt * MINE, MINE, axis=1)
    out = place(0, first)
    return place(1, second, out), energy


def solution(mesh):
    placed = (
        P("pair", None, None, None),
        P(None, None, None, ("virt", "pair")),
        P(),
        P(),
        P("pair", None, None),
        P(),
        P(),
    )
    return jax.shard_map(
        shards,
        mesh=mesh,
        in_specs=placed,
        out_specs=(P("pair", None, "virt"), P("pair", "virt")),
        check_vma=False,
    )
```

```python
import jax
import jax.numpy as jnp
from jax import lax
from jax.experimental import pallas as pl
from jax.experimental.pallas import tpu as pltpu
from jax.sharding import PartitionSpec as P

IRREPS = 8
NV = 512
BLK = 64
SLABS = 2
PCAP = 1024
KQ = 256
KS = 1024
VIRTS = 64
OWN = NV // VIRTS
MINE = PCAP // VIRTS
VMEM = 20 * 1024 * 1024
ABLK = 256
SUB = 32
RBLK = 256
EXTRA = 128


def iota(shape, axis):
    return lax.broadcasted_iota(jnp.int32, shape, axis)


def regroup_kernel(pair_ref, x_ref, even, own, plus, far, minus, perm, held):
    rows = SUB * IRREPS

    @pl.when((pl.program_id(0) == 0) & (pl.program_id(1) == 0))
    def _():
        to, source = iota((rows, rows), 0), iota((rows, rows), 1)
        at = (to & (SUB - 1)) * IRREPS + (to >> 5)
        perm[...] = jnp.where(at == source, 1.0, 0.0).astype(jnp.bfloat16)

    for sub in range(ABLK // SUB):
        block = x_ref[0, sub * rows : (sub + 1) * rows, :]
        moved = jnp.dot(perm[...], block, preferred_element_type=jnp.float32).astype(jnp.bfloat16)
        at = slice(sub * SUB, (sub + 1) * SUB)
        for pair in range(4):
            even[pair, 0, at, :] = moved[(2 * pair) * SUB : (2 * pair + 1) * SUB]
            held[pair, at, :] = moved[(2 * pair + 1) * SUB : (2 * pair + 2) * SUB]
    me = pair_ref[0]
    own[0] = held[me]
    plus[0] = held[(me + 1) % 4]
    far[0] = held[(me + 2) % 4]
    minus[0] = held[(me + 3) % 4]


def regroup(pair_id, integrals):
    each = pltpu.HBM((SLABS, NV, KQ), jnp.bfloat16)
    spec = pl.BlockSpec((1, ABLK, KQ), lambda s, i, me: (s, i, 0))
    return pl.pallas_call(
        regroup_kernel,
        grid_spec=pltpu.PrefetchScalarGridSpec(
            num_scalar_prefetch=1,
            grid=(SLABS, NV // ABLK),
            in_specs=[pl.BlockSpec((1, ABLK * IRREPS, KQ), lambda s, i, me: (s, i, 0))],
            out_specs=[pl.BlockSpec((4, 1, ABLK, KQ), lambda s, i, me: (0, s, i, 0))] + [spec] * 4,
            scratch_shapes=[
                pltpu.VMEM((SUB * IRREPS, SUB * IRREPS), jnp.bfloat16),
                pltpu.VMEM((4, ABLK, KQ), jnp.bfloat16),
            ],
        ),
        out_shape=[pltpu.HBM((4, SLABS, NV, KQ), jnp.bfloat16)] + [each] * 4,
        compiler_params=pltpu.CompilerParams(vmem_limit_bytes=3 * VMEM),
        name="regroup",
    )(pair_id, integrals.reshape(SLABS, NV * IRREPS, KQ))


def ladder_kernel(parity, ids, virt_counts, pair_counts, eps, *refs):
    if parity == 0:
        pieces, (amp, eps_a, occ, send, energy, held, stage, sems) = refs[:-8], refs[-8:]
    else:
        pieces, (amp, eps_a, occ, energy0, send, held, stage, sems, energy, extra) = refs[:-10], refs[-10:]
    me, virt = ids[0], ids[1]
    h = 2 * me + parity
    mask = jnp.where((iota((1, KQ), 1) & (BLK - 1)) < virt_counts[h], 1.0, 0.0).astype(jnp.bfloat16)
    for slab in range(SLABS):
        if parity == 0:
            for source in range(4):
                to = slab * KS + source * KQ
                held[:, to : to + KQ] = pieces[0][source, slab] * mask
        else:
            for shift, piece in zip((0, 3, 2, 1), pieces):
                to = pl.multiple_of(slab * KS + ((me + shift) % 4) * KQ, KQ)
                held[:, pl.ds(to, KQ)] = piece[slab] * mask
    slot = iota((BLK, RBLK), 0)
    column = iota((BLK, RBLK), 1)
    copies = []
    for block in range(PCAP // RBLK):
        at = slice(block * RBLK, (block + 1) * RBLK)
        total = None
        for slab in range(SLABS):
            term = lax.dot_general(
                held[:, slab * KS : (slab + 1) * KS],
                amp[slab, at, :],
                (((1,), (1,)), ((), ())),
                preferred_element_type=jnp.float32,
            )
            total = term if total is None else total + term
        occ_row = occ[parity : parity + 1, at]
        live_row = block * RBLK + column < pair_counts[h]
        summed = jnp.zeros((1, RBLK), jnp.float32)
        for ha in range(IRREPS):
            rows = slice(ha * BLK, (ha + 1) * BLK)
            hb = jnp.bitwise_xor(h, ha)
            part = total[rows]
            denom = (eps_a[rows, :] + eps[hb * BLK + virt]) - occ_row
            live_a = jnp.where(virt < virt_counts[hb], virt_counts[ha], 0)
            ratio = jnp.where((slot < live_a) & live_row, part / denom, 0.0)
            summed = summed + jnp.sum(ratio * part, axis=0, keepdims=True)
            stage[block, rows, :] = ratio.astype(jnp.bfloat16)
        energy[:, at] = summed / (NV * BLK)
        copy = pltpu.make_async_copy(stage.at[block], send.at[:, pl.ds(block * RBLK, RBLK)], sems.at[block])
        copy.start()
        copies.append(copy)
    if parity == 1:
        value = jnp.concatenate([energy0[...], energy[...]], axis=0)
        high = value.astype(jnp.bfloat16).astype(jnp.float32)
        rest = value - high
        middle = rest.astype(jnp.bfloat16).astype(jnp.float32)
        low = rest - middle
        terms = jnp.concatenate([high, middle, low, jnp.zeros((2, PCAP), jnp.float32)], axis=0)
        spread = jnp.broadcast_to(terms[None], (VIRTS, OWN, PCAP)).reshape(NV, PCAP)
        owner = (iota((NV, PCAP), 1) // MINE) == (iota((NV, PCAP), 0) // OWN)
        spread = jnp.where(owner, spread, 0.0).astype(jnp.bfloat16)
        lane = (iota((PCAP, EXTRA), 0) & (MINE - 1)) == iota((PCAP, EXTRA), 1)
        select = jnp.where(lane, 1.0, 0.0).astype(jnp.bfloat16)
        extra[...] = jnp.dot(spread, select, preferred_element_type=jnp.float32).astype(jnp.bfloat16)
        copy = pltpu.make_async_copy(extra, send.at[:, pl.ds(PCAP, EXTRA)], sems.at[PCAP // RBLK])
        copy.start()
        copies.append(copy)
    for copy in copies:
        copy.wait()


def ladder(parity, scalars, pieces, amp, eps_a, occ, *energy0):
    vmem = pl.BlockSpec(memory_space=pltpu.VMEM)
    columns = PCAP if parity == 0 else PCAP + EXTRA
    row = jax.ShapeDtypeStruct((1, PCAP), jnp.float32)
    scratch = [
        pltpu.VMEM((NV, SLABS * KS), jnp.bfloat16),
        pltpu.VMEM((PCAP // RBLK, NV, RBLK), jnp.bfloat16),
        pltpu.SemaphoreType.DMA((PCAP // RBLK + 1,)),
    ]
    if parity == 1:
        scratch += [pltpu.VMEM((1, PCAP), jnp.float32), pltpu.VMEM((NV, EXTRA), jnp.bfloat16)]
    return pl.pallas_call(
        lambda *refs: ladder_kernel(parity, *refs),
        in_specs=[pl.BlockSpec(memory_space=pltpu.SMEM)] * 4 + [vmem] * (len(pieces) + 3 + len(energy0)),
        out_specs=[pl.BlockSpec(memory_space=pl.ANY)] + [vmem] * (1 - parity),
        out_shape=[jax.ShapeDtypeStruct((NV, columns), jnp.bfloat16)] + [row] * (1 - parity),
        scratch_shapes=scratch,
        compiler_params=pltpu.CompilerParams(vmem_limit_bytes=VMEM),
        cost_estimate=pl.CostEstimate(
            flops=2 * NV * PCAP * SLABS * KS, bytes_accessed=7 << 20, transcendentals=0
        ),
        name="ladder",
    )(*scalars, *pieces, amp, eps_a, occ, *energy0)


def put(block, out, perm):
    @pl.when(pl.program_id(0) == 0)
    def _():
        source, to = iota((NV, NV), 0), iota((NV, NV), 1)
        at = (source & (OWN - 1)) * BLK + (source >> 3)
        perm[...] = jnp.where(at == to, 1.0, 0.0).astype(jnp.bfloat16)

    out[0] = lax.dot_general(
        block[...], perm[...], (((0,), (0,)), ((), ())), preferred_element_type=jnp.float32
    ).astype(jnp.bfloat16)


def place_even_kernel(block, out, perm):
    put(block, out, perm)


def place_odd_kernel(block, extra, before, out, energy, perm):
    put(block, out, perm)

    @pl.when(pl.program_id(0) == 0)
    def _():
        values = extra[...].astype(jnp.float32)
        kind = iota((NV, EXTRA), 0) & (OWN - 1)
        for parity in range(2):
            mine = (kind < 6) & ((kind & 1) == parity)
            summed = jnp.sum(jnp.where(mine, values, 0.0), axis=0, keepdims=True)
            energy[parity : parity + 1, :] = summed[:, :MINE]


def place(parity, block, before=None):
    in_specs = [pl.BlockSpec((NV, RBLK), lambda i: (0, i))]
    out_spec = pl.BlockSpec((1, RBLK, NV), lambda i: (parity, i, 0))
    out = jax.ShapeDtypeStruct((2, PCAP, NV), jnp.bfloat16)
    common = dict(
        grid=(PCAP // RBLK,),
        scratch_shapes=[pltpu.VMEM((NV, NV), jnp.bfloat16)],
        compiler_params=pltpu.CompilerParams(vmem_limit_bytes=VMEM),
        cost_estimate=pl.CostEstimate(flops=2 * NV * NV * PCAP, bytes_accessed=2 << 20, transcendentals=0),
        name="place",
    )
    if parity == 0:
        return pl.pallas_call(place_even_kernel, in_specs=in_specs, out_specs=out_spec, out_shape=out, **common)(block)
    in_specs += [
        pl.BlockSpec((NV, EXTRA), lambda i: (0, PCAP // EXTRA)),
        pl.BlockSpec(memory_space=pl.ANY),
    ]
    return pl.pallas_call(
        place_odd_kernel,
        in_specs=in_specs,
        out_specs=[out_spec, pl.BlockSpec((2, MINE), lambda i: (0, 0))],
        out_shape=[out, jax.ShapeDtypeStruct((2, MINE), jnp.float32)],
        input_output_aliases={2: 0},
        **common,
    )(block, block, before)


def pick(ids, table):
    onehot = ids[..., None] == jnp.arange(table.shape[0], dtype=jnp.int32)
    return jnp.sum(jnp.where(onehot, table, 0), axis=-1)


def step(value, by):
    return lax.ppermute(value, "pair", [(i, (i + by) % 4) for i in range(4)])


def across(value):
    return lax.all_to_all(value, "virt", 0, 0, tiled=True)


def shards(amplitudes, integrals, virt_counts, pair_counts, pair_list, eps_occ, eps_virt):
    me = lax.axis_index("pair").astype(jnp.int32)
    virt = lax.axis_index("virt").astype(jnp.int32)
    even, own, plus, far, minus = regroup(me[None], integrals)
    even = lax.all_to_all(even, "pair", 0, 0, tiled=True)

    amp = [jnp.transpose(amplitudes[parity], (1, 0, 2)) for parity in range(2)]
    occ_terms = pick(pair_list, eps_occ)
    occ = occ_terms[:, :, 0] + occ_terms[:, :, 1]
    eps_a = eps_virt[:, None]
    scalars = (jnp.stack([me, virt]), virt_counts, pair_counts, eps_virt)

    even, plus, far, minus = lax.optimization_barrier((even, plus, far, minus))
    left, far, right = step(plus, 1), step(far, 2), step(minus, 3)
    send, energy0 = ladder(0, scalars, (even,), amp[0], eps_a, occ)
    first = across(send)
    (send,) = ladder(1, scalars, (own, left, far, right), amp[1], eps_a, occ, energy0)
    first, send = lax.optimization_barrier((first, send))
    second = across(send)
    out = place(0, first)
    return tuple(place(1, second, out))


def solution(mesh):
    placed = (
        P("pair", None, None, None),
        P(None, None, None, ("virt", "pair")),
        P(),
        P(),
        P("pair", None, None),
        P(),
        P(),
    )
    return jax.shard_map(
        shards,
        mesh=mesh,
        in_specs=placed,
        out_specs=(P("pair", None, "virt"), P("pair", "virt")),
        check_vma=False,
    )
```

```python
import jax
import jax.numpy as jnp
from jax import lax
from jax.experimental import pallas as pl
from jax.experimental.pallas import tpu as pltpu
from jax.sharding import PartitionSpec as P

IRREPS = 8
NV = 512
BLK = 64
SLABS = 2
PCAP = 1024
KQ = 256
KS = 1024
VIRTS = 64
OWN = NV // VIRTS
MINE = PCAP // VIRTS
VMEM = 20 * 1024 * 1024
ABLK = 256
SUB = 32
RBLK = 256
EXTRA = 128


def iota(shape, axis):
    return lax.broadcasted_iota(jnp.int32, shape, axis)


def regroup_kernel(parity, pair_ref, x_ref, *refs):
    outs, (perm, held) = refs[:-2], refs[-2:]
    rows = SUB * IRREPS

    @pl.when((pl.program_id(0) == 0) & (pl.program_id(1) == 0))
    def _():
        to, source = iota((rows // 2, rows), 0), iota((rows // 2, rows), 1)
        at = (to & (SUB - 1)) * IRREPS + 2 * (to >> 5) + parity
        perm[...] = jnp.where(at == source, 1.0, 0.0).astype(jnp.bfloat16)

    for sub in range(ABLK // SUB):
        block = x_ref[0, sub * rows : (sub + 1) * rows, :]
        moved = jnp.dot(perm[...], block, preferred_element_type=jnp.float32).astype(jnp.bfloat16)
        at = slice(sub * SUB, (sub + 1) * SUB)
        for pair in range(4):
            piece = moved[pair * SUB : (pair + 1) * SUB]
            if parity == 0:
                outs[0][pair, 0, at, :] = piece
            else:
                held[pair, at, :] = piece
    if parity == 1:
        me = pair_ref[0]
        for shift in range(4):
            outs[shift][0] = held[(me + shift) % 4]


def regroup(parity, pair_id, integrals):
    if parity == 0:
        specs = [pl.BlockSpec((4, 1, ABLK, KQ), lambda s, i, me: (0, s, i, 0))]
        shapes = [pltpu.HBM((4, SLABS, NV, KQ), jnp.bfloat16)]
    else:
        specs = [pl.BlockSpec((1, ABLK, KQ), lambda s, i, me: (s, i, 0))] * 4
        shapes = [pltpu.HBM((SLABS, NV, KQ), jnp.bfloat16)] * 4
    return pl.pallas_call(
        lambda *refs: regroup_kernel(parity, *refs),
        grid_spec=pltpu.PrefetchScalarGridSpec(
            num_scalar_prefetch=1,
            grid=(SLABS, NV // ABLK),
            in_specs=[pl.BlockSpec((1, ABLK * IRREPS, KQ), lambda s, i, me: (s, i, 0))],
            out_specs=specs,
            scratch_shapes=[
                pltpu.VMEM((SUB * IRREPS // 2, SUB * IRREPS), jnp.bfloat16),
                pltpu.VMEM((4, ABLK, KQ), jnp.bfloat16),
            ],
        ),
        out_shape=shapes,
        compiler_params=pltpu.CompilerParams(vmem_limit_bytes=3 * VMEM),
        cost_estimate=pl.CostEstimate(flops=1 << 30, bytes_accessed=6 << 20, transcendentals=0),
        name="regroup",
    )(pair_id, integrals.reshape(SLABS, NV * IRREPS, KQ))


def ladder_kernel(parity, ids, virt_counts, pair_counts, eps, *refs):
    if parity == 0:
        pieces, (amp_hbm, eps_a, occ, send, energy, held, stage, sems, amp, loads) = refs[:-10], refs[-10:]
    else:
        pieces, (amp_hbm, eps_a, occ, energy0, send, held, stage, sems, amp, loads, energy, extra) = (
            refs[:-12],
            refs[-12:],
        )
    fetches = []
    for block in range(PCAP // RBLK):
        rows = pl.ds(block * RBLK, RBLK)
        fetches.append(pltpu.make_async_copy(amp_hbm.at[:, rows, :], amp.at[:, rows, :], loads.at[block]))
        fetches[-1].start()
    me, virt = ids[0], ids[1]
    h = 2 * me + parity
    mask = jnp.where((iota((1, KQ), 1) & (BLK - 1)) < virt_counts[h], 1.0, 0.0).astype(jnp.bfloat16)
    for slab in range(SLABS):
        if parity == 0:
            for source in range(4):
                to = slab * KS + source * KQ
                held[:, to : to + KQ] = pieces[0][source, slab] * mask
        else:
            for shift, piece in zip((0, 3, 2, 1), pieces):
                to = pl.multiple_of(slab * KS + ((me + shift) % 4) * KQ, KQ)
                held[:, pl.ds(to, KQ)] = piece[slab] * mask
    slot = iota((BLK, RBLK), 0)
    column = iota((BLK, RBLK), 1)
    copies = []
    for block in range(PCAP // RBLK):
        at = slice(block * RBLK, (block + 1) * RBLK)
        fetches[block].wait()
        total = None
        for slab in range(SLABS):
            term = lax.dot_general(
                held[:, slab * KS : (slab + 1) * KS],
                amp[slab, at, :],
                (((1,), (1,)), ((), ())),
                preferred_element_type=jnp.float32,
            )
            total = term if total is None else total + term
        occ_row = occ[parity : parity + 1, at]
        live_row = block * RBLK + column < pair_counts[h]
        summed = jnp.zeros((1, RBLK), jnp.float32)
        for ha in range(IRREPS):
            rows = slice(ha * BLK, (ha + 1) * BLK)
            hb = jnp.bitwise_xor(h, ha)
            part = total[rows]
            denom = (eps_a[rows, :] + eps[hb * BLK + virt]) - occ_row
            live_a = jnp.where(virt < virt_counts[hb], virt_counts[ha], 0)
            ratio = jnp.where((slot < live_a) & live_row, part / denom, 0.0)
            summed = summed + jnp.sum(ratio * part, axis=0, keepdims=True)
            stage[block, rows, :] = ratio.astype(jnp.bfloat16)
        energy[:, at] = summed / (NV * BLK)
        copy = pltpu.make_async_copy(stage.at[block], send.at[:, pl.ds(block * RBLK, RBLK)], sems.at[block])
        copy.start()
        copies.append(copy)
    if parity == 1:
        value = jnp.concatenate([energy0[...], energy[...]], axis=0)
        high = value.astype(jnp.bfloat16).astype(jnp.float32)
        rest = value - high
        middle = rest.astype(jnp.bfloat16).astype(jnp.float32)
        low = rest - middle
        terms = jnp.concatenate([high, middle, low, jnp.zeros((2, PCAP), jnp.float32)], axis=0)
        spread = jnp.broadcast_to(terms[None], (VIRTS, OWN, PCAP)).reshape(NV, PCAP)
        owner = (iota((NV, PCAP), 1) // MINE) == (iota((NV, PCAP), 0) // OWN)
        spread = jnp.where(owner, spread, 0.0).astype(jnp.bfloat16)
        lane = (iota((PCAP, EXTRA), 0) & (MINE - 1)) == iota((PCAP, EXTRA), 1)
        select = jnp.where(lane, 1.0, 0.0).astype(jnp.bfloat16)
        extra[...] = jnp.dot(spread, select, preferred_element_type=jnp.float32).astype(jnp.bfloat16)
        copy = pltpu.make_async_copy(extra, send.at[:, pl.ds(PCAP, EXTRA)], sems.at[PCAP // RBLK])
        copy.start()
        copies.append(copy)
    for copy in copies:
        copy.wait()


def ladder(parity, scalars, pieces, amp, eps_a, occ, *energy0):
    vmem = pl.BlockSpec(memory_space=pltpu.VMEM)
    columns = PCAP if parity == 0 else PCAP + EXTRA
    row = jax.ShapeDtypeStruct((1, PCAP), jnp.float32)
    scratch = [
        pltpu.VMEM((NV, SLABS * KS), jnp.bfloat16),
        pltpu.VMEM((PCAP // RBLK, NV, RBLK), jnp.bfloat16),
        pltpu.SemaphoreType.DMA((PCAP // RBLK + 1,)),
        pltpu.VMEM((SLABS, PCAP, KS), jnp.bfloat16),
        pltpu.SemaphoreType.DMA((PCAP // RBLK,)),
    ]
    if parity == 1:
        scratch += [pltpu.VMEM((1, PCAP), jnp.float32), pltpu.VMEM((NV, EXTRA), jnp.bfloat16)]
    return pl.pallas_call(
        lambda *refs: ladder_kernel(parity, *refs),
        in_specs=[pl.BlockSpec(memory_space=pltpu.SMEM)] * 4
        + [vmem] * len(pieces)
        + [pl.BlockSpec(memory_space=pltpu.HBM)]
        + [vmem] * (2 + len(energy0)),
        out_specs=[pl.BlockSpec(memory_space=pl.ANY)] + [vmem] * (1 - parity),
        out_shape=[jax.ShapeDtypeStruct((NV, columns), jnp.bfloat16)] + [row] * (1 - parity),
        scratch_shapes=scratch,
        compiler_params=pltpu.CompilerParams(vmem_limit_bytes=VMEM),
        cost_estimate=pl.CostEstimate(
            flops=(1 + parity * 8) * 2 * NV * PCAP * SLABS * KS, bytes_accessed=7 << 20, transcendentals=0
        ),
        name="ladder",
    )(*scalars, *pieces, pltpu.with_memory_space_constraint(amp, pltpu.HBM), eps_a, occ, *energy0)


def put(block, out, perm):
    @pl.when(pl.program_id(0) == 0)
    def _():
        source, to = iota((NV, NV), 0), iota((NV, NV), 1)
        at = (source & (OWN - 1)) * BLK + (source >> 3)
        perm[...] = jnp.where(at == to, 1.0, 0.0).astype(jnp.bfloat16)

    out[0] = lax.dot_general(
        block[...], perm[...], (((0,), (0,)), ((), ())), preferred_element_type=jnp.float32
    ).astype(jnp.bfloat16)


def place_even_kernel(block, out, perm):
    put(block, out, perm)


def place_odd_kernel(block, extra, before, out, energy, perm):
    put(block, out, perm)

    @pl.when(pl.program_id(0) == 0)
    def _():
        values = extra[...].astype(jnp.float32)
        kind = iota((NV, EXTRA), 0) & (OWN - 1)
        for parity in range(2):
            mine = (kind < 6) & ((kind & 1) == parity)
            summed = jnp.sum(jnp.where(mine, values, 0.0), axis=0, keepdims=True)
            energy[parity : parity + 1, :] = summed[:, :MINE]


def place(parity, block, before=None):
    in_specs = [pl.BlockSpec((NV, RBLK), lambda i: (0, i))]
    out_spec = pl.BlockSpec((1, RBLK, NV), lambda i: (parity, i, 0))
    out = jax.ShapeDtypeStruct((2, PCAP, NV), jnp.bfloat16)
    common = dict(
        grid=(PCAP // RBLK,),
        scratch_shapes=[pltpu.VMEM((NV, NV), jnp.bfloat16)],
        compiler_params=pltpu.CompilerParams(vmem_limit_bytes=VMEM),
        cost_estimate=pl.CostEstimate(flops=2 * NV * NV * PCAP, bytes_accessed=2 << 20, transcendentals=0),
        name="place",
    )
    if parity == 0:
        return pl.pallas_call(place_even_kernel, in_specs=in_specs, out_specs=out_spec, out_shape=out, **common)(block)
    in_specs += [
        pl.BlockSpec((NV, EXTRA), lambda i: (0, PCAP // EXTRA)),
        pl.BlockSpec(memory_space=pl.ANY),
    ]
    return pl.pallas_call(
        place_odd_kernel,
        in_specs=in_specs,
        out_specs=[out_spec, pl.BlockSpec((2, MINE), lambda i: (0, 0))],
        out_shape=[out, jax.ShapeDtypeStruct((2, MINE), jnp.float32)],
        input_output_aliases={2: 0},
        **common,
    )(block, block, before)


def pick(ids, table):
    onehot = ids[..., None] == jnp.arange(table.shape[0], dtype=jnp.int32)
    return jnp.sum(jnp.where(onehot, table, 0), axis=-1)


def step(value, by):
    return lax.ppermute(value, "pair", [(i, (i + by) % 4) for i in range(4)])


def across(value):
    return lax.all_to_all(value, "virt", 0, 0, tiled=True)


def shards(amplitudes, integrals, virt_counts, pair_counts, pair_list, eps_occ, eps_virt):
    me = lax.axis_index("pair").astype(jnp.int32)
    virt = lax.axis_index("virt").astype(jnp.int32)
    (even,) = regroup(0, me[None], integrals)
    own, plus, far, minus = regroup(1, me[None], integrals)
    even = lax.all_to_all(even, "pair", 0, 0, tiled=True)

    amp = [jnp.transpose(amplitudes[parity], (1, 0, 2)) for parity in range(2)]
    occ_terms = pick(pair_list, eps_occ)
    occ = occ_terms[:, :, 0] + occ_terms[:, :, 1]
    eps_a = eps_virt[:, None]
    scalars = (jnp.stack([me, virt]), virt_counts, pair_counts, eps_virt)

    even, plus, far, minus = lax.optimization_barrier((even, plus, far, minus))
    left, far, right = step(plus, 1), step(far, 2), step(minus, 3)
    send, energy0 = ladder(0, scalars, (even,), amp[0], eps_a, occ)
    first = across(send)
    (send,) = ladder(1, scalars, (own, left, far, right), amp[1], eps_a, occ, energy0)
    first, send = lax.optimization_barrier((first, send))
    second = across(send)
    out = place(0, first)
    return tuple(place(1, second, out))


def solution(mesh):
    placed = (
        P("pair", None, None, None),
        P(None, None, None, ("virt", "pair")),
        P(),
        P(),
        P("pair", None, None),
        P(),
        P(),
    )
    return jax.shard_map(
        shards,
        mesh=mesh,
        in_specs=placed,
        out_specs=(P("pair", None, "virt"), P("pair", "virt")),
        check_vma=False,
    )
```

```python
import jax
import jax.numpy as jnp
from jax import lax
from jax.experimental import pallas as pl
from jax.experimental.pallas import tpu as pltpu
from jax.sharding import PartitionSpec as P

IRREPS = 8
NV = 512
BLK = 64
SLABS = 2
PCAP = 1024
KQ = 256
KS = 1024
VIRTS = 64
OWN = NV // VIRTS
MINE = PCAP // VIRTS
VMEM = 20 * 1024 * 1024
ABLK = 256
SUB = 32
RBLK = 512
EXTRA = 128


def iota(shape, axis):
    return lax.broadcasted_iota(jnp.int32, shape, axis)


def regroup_kernel(parity, pair_ref, x_hbm, *refs):
    outs, (x, held, loads, stores) = refs[:-4], refs[-4:]
    parts = [(slab, block) for slab in range(SLABS) for block in range(NV // ABLK)]
    fetches = []
    for slab, block in parts:
        at = pl.ds(block * ABLK * IRREPS, ABLK * IRREPS)
        fetch = pltpu.make_async_copy(x_hbm.at[slab, at, :], x.at[slab, at, :], loads.at[slab, block])
        fetch.start()
        fetches.append(fetch)
    rows = SUB * IRREPS
    to, source = iota((rows // 2, rows), 0), iota((rows // 2, rows), 1)
    perm = jnp.where((to & (SUB - 1)) * IRREPS + 2 * (to >> 5) + parity == source, 1.0, 0.0).astype(jnp.bfloat16)
    copies = []
    for fetch, (slab, block) in zip(fetches, parts):
        fetch.wait()
        for sub in range(ABLK // SUB):
            first = block * ABLK + sub * SUB
            moved = jnp.dot(
                perm,
                x[slab, first * IRREPS : first * IRREPS + rows, :],
                preferred_element_type=jnp.float32,
            ).astype(jnp.bfloat16)
            for pair in range(4):
                held[pair, slab, first : first + SUB, :] = moved[pair * SUB : (pair + 1) * SUB]
        if parity == 0:
            at = pl.ds(block * ABLK, ABLK)
            copy = pltpu.make_async_copy(
                held.at[:, slab, at, :], outs[0].at[:, slab, at, :], stores.at[slab * (NV // ABLK) + block]
            )
            copy.start()
            copies.append(copy)
    if parity == 1:
        me = pair_ref[0]
        for shift in range(4):
            copy = pltpu.make_async_copy(held.at[(me + shift) % 4], outs[shift], stores.at[shift])
            copy.start()
            copies.append(copy)
    for copy in copies:
        copy.wait()


def regroup(parity, pair_id, integrals):
    if parity == 0:
        shapes = [pltpu.HBM((4, SLABS, NV, KQ), jnp.bfloat16)]
    else:
        shapes = [pltpu.HBM((SLABS, NV, KQ), jnp.bfloat16)] * 4
    flat = pltpu.with_memory_space_constraint(integrals.reshape(SLABS, NV * IRREPS, KQ), pltpu.HBM)
    return pl.pallas_call(
        lambda *refs: regroup_kernel(parity, *refs),
        in_specs=[pl.BlockSpec(memory_space=pltpu.SMEM), pl.BlockSpec(memory_space=pltpu.HBM)],
        out_specs=[pl.BlockSpec(memory_space=pltpu.HBM)] * len(shapes),
        out_shape=shapes,
        scratch_shapes=[
            pltpu.VMEM((SLABS, NV * IRREPS, KQ), jnp.bfloat16),
            pltpu.VMEM((4, SLABS, NV, KQ), jnp.bfloat16),
            pltpu.SemaphoreType.DMA((SLABS, NV // ABLK)),
            pltpu.SemaphoreType.DMA((SLABS * (NV // ABLK),)),
        ],
        compiler_params=pltpu.CompilerParams(vmem_limit_bytes=VMEM),
        cost_estimate=pl.CostEstimate(flops=1 << 30, bytes_accessed=6 << 20, transcendentals=0),
        name="regroup",
    )(pair_id, flat)


def ladder_kernel(parity, ids, virt_counts, pair_counts, eps, *refs):
    if parity == 0:
        pieces, (amp, eps_a, occ, send, energy_out, held, stage, sems, energy) = refs[:-9], refs[-9:]
    else:
        pieces, (amp, eps_a, occ, energy0, send, held, stage, sems, energy, extra) = refs[:-10], refs[-10:]
    me, virt = ids[0], ids[1]
    h = 2 * me + parity
    mask = jnp.where((iota((1, KQ), 1) & (BLK - 1)) < virt_counts[h], 1.0, 0.0).astype(jnp.bfloat16)
    for slab in range(SLABS):
        if parity == 0:
            for source in range(4):
                to = slab * KS + source * KQ
                held[:, to : to + KQ] = pieces[0][source, slab] * mask
        else:
            for shift, piece in zip((0, 3, 2, 1), pieces):
                to = pl.multiple_of(slab * KS + ((me + shift) % 4) * KQ, KQ)
                held[:, pl.ds(to, KQ)] = piece[slab] * mask
    slot = iota((BLK, RBLK), 0)
    column = iota((BLK, RBLK), 1)
    copies = []
    for block in range(PCAP // RBLK):
        at = slice(block * RBLK, (block + 1) * RBLK)
        total = None
        for slab in range(SLABS):
            term = lax.dot_general(
                held[:, slab * KS : (slab + 1) * KS],
                amp[slab, at, :],
                (((1,), (1,)), ((), ())),
                preferred_element_type=jnp.float32,
            )
            total = term if total is None else total + term
        occ_row = occ[parity : parity + 1, at]
        live_row = block * RBLK + column < pair_counts[h]
        summed = jnp.zeros((1, RBLK), jnp.float32)
        for ha in range(IRREPS):
            rows = slice(ha * BLK, (ha + 1) * BLK)
            hb = jnp.bitwise_xor(h, ha)
            part = total[rows]
            denom = (eps_a[rows, :] + eps[hb * BLK + virt]) - occ_row
            live_a = jnp.where(virt < virt_counts[hb], virt_counts[ha], 0)
            ratio = jnp.where((slot < live_a) & live_row, part / denom, 0.0)
            summed = summed + jnp.sum(ratio * part, axis=0, keepdims=True)
            stage[block, rows, :] = ratio.astype(jnp.bfloat16)
        energy[:, at] = summed / (NV * BLK)
        copy = pltpu.make_async_copy(stage.at[block], send.at[:, pl.ds(block * RBLK, RBLK)], sems.at[block])
        copy.start()
        copies.append(copy)
    if parity == 0:
        copy = pltpu.make_async_copy(energy, energy_out, sems.at[PCAP // RBLK])
        copy.start()
        copies.append(copy)
    else:
        value = jnp.concatenate([energy0[...], energy[...]], axis=0)
        high = value.astype(jnp.bfloat16).astype(jnp.float32)
        rest = value - high
        middle = rest.astype(jnp.bfloat16).astype(jnp.float32)
        low = rest - middle
        terms = jnp.concatenate([high, middle, low, jnp.zeros((2, PCAP), jnp.float32)], axis=0)
        spread = jnp.broadcast_to(terms[None], (VIRTS, OWN, PCAP)).reshape(NV, PCAP)
        owner = (iota((NV, PCAP), 1) // MINE) == (iota((NV, PCAP), 0) // OWN)
        spread = jnp.where(owner, spread, 0.0).astype(jnp.bfloat16)
        lane = (iota((PCAP, EXTRA), 0) & (MINE - 1)) == iota((PCAP, EXTRA), 1)
        select = jnp.where(lane, 1.0, 0.0).astype(jnp.bfloat16)
        extra[...] = jnp.dot(spread, select, preferred_element_type=jnp.float32).astype(jnp.bfloat16)
        copy = pltpu.make_async_copy(extra, send.at[:, pl.ds(PCAP, EXTRA)], sems.at[PCAP // RBLK])
        copy.start()
        copies.append(copy)
    for copy in copies:
        copy.wait()


def ladder(parity, scalars, pieces, amp, eps_a, occ, *energy0):
    vmem = pl.BlockSpec(memory_space=pltpu.VMEM)
    columns = PCAP if parity == 0 else PCAP + EXTRA
    row = pltpu.HBM((1, PCAP), jnp.float32)
    scratch = [
        pltpu.VMEM((NV, SLABS * KS), jnp.bfloat16),
        pltpu.VMEM((PCAP // RBLK, NV, RBLK), jnp.bfloat16),
        pltpu.SemaphoreType.DMA((PCAP // RBLK + 1,)),
        pltpu.VMEM((1, PCAP), jnp.float32),
    ]
    if parity == 1:
        scratch.append(pltpu.VMEM((NV, EXTRA), jnp.bfloat16))
    return pl.pallas_call(
        lambda *refs: ladder_kernel(parity, *refs),
        in_specs=[pl.BlockSpec(memory_space=pltpu.SMEM)] * 4
        + [vmem] * (len(pieces) + 3 + len(energy0)),
        out_specs=[pl.BlockSpec(memory_space=pltpu.HBM)] * (2 - parity),
        out_shape=[pltpu.HBM((NV, columns), jnp.bfloat16)] + [row] * (1 - parity),
        scratch_shapes=scratch,
        compiler_params=pltpu.CompilerParams(vmem_limit_bytes=VMEM),
        cost_estimate=pl.CostEstimate(
            flops=(1 + parity * 8) * 2 * NV * PCAP * SLABS * KS, bytes_accessed=7 << 20, transcendentals=0
        ),
        name="ladder",
    )(*scalars, *pieces, amp, eps_a, occ, *energy0)


def place_kernel(parity, block, *refs):
    if parity == 0:
        out, stage, sems = refs
    else:
        _, out, energy, stage, sems = refs
    source, to = iota((NV, NV), 0), iota((NV, NV), 1)
    perm = jnp.where((source & (OWN - 1)) * BLK + (source >> 3) == to, 1.0, 0.0).astype(jnp.bfloat16)
    copies = []
    for part in range(PCAP // RBLK):
        stage[part] = lax.dot_general(
            block[:, part * RBLK : (part + 1) * RBLK],
            perm,
            (((0,), (0,)), ((), ())),
            preferred_element_type=jnp.float32,
        ).astype(jnp.bfloat16)
        copy = pltpu.make_async_copy(stage.at[part], out.at[parity, pl.ds(part * RBLK, RBLK), :], sems.at[part])
        copy.start()
        copies.append(copy)
    if parity == 1:
        values = block[:, PCAP : PCAP + EXTRA].astype(jnp.float32)
        kind = iota((NV, EXTRA), 0) & (OWN - 1)
        for which in range(2):
            mine = (kind < 6) & ((kind & 1) == which)
            summed = jnp.sum(jnp.where(mine, values, 0.0), axis=0, keepdims=True)
            energy[which : which + 1, :] = summed[:, :MINE]
    for copy in copies:
        copy.wait()


def place(parity, block, *before):
    vmem = pl.BlockSpec(memory_space=pltpu.VMEM)
    hbm = pl.BlockSpec(memory_space=pl.ANY)
    out = jax.ShapeDtypeStruct((2, PCAP, NV), jnp.bfloat16)
    return pl.pallas_call(
        lambda *refs: place_kernel(parity, *refs),
        in_specs=[vmem] + [hbm] * parity,
        out_specs=[hbm] + [vmem] * parity,
        out_shape=[out] + [jax.ShapeDtypeStruct((2, MINE), jnp.float32)] * parity,
        input_output_aliases={1: 0} if parity else {},
        scratch_shapes=[
            pltpu.VMEM((PCAP // RBLK, RBLK, NV), jnp.bfloat16),
            pltpu.SemaphoreType.DMA((PCAP // RBLK,)),
        ],
        compiler_params=pltpu.CompilerParams(vmem_limit_bytes=VMEM),
        cost_estimate=pl.CostEstimate(flops=2 * NV * NV * PCAP, bytes_accessed=2 << 20, transcendentals=0),
        name="place",
    )(block, *before)


def pick(ids, table):
    onehot = ids[..., None] == jnp.arange(table.shape[0], dtype=jnp.int32)
    return jnp.sum(jnp.where(onehot, table, 0), axis=-1)


def step(value, by):
    return lax.ppermute(value, "pair", [(i, (i + by) % 4) for i in range(4)])


def across(value):
    return lax.all_to_all(value, "virt", 0, 0, tiled=True)


def shards(amplitudes, integrals, virt_counts, pair_counts, pair_list, eps_occ, eps_virt):
    me = lax.axis_index("pair").astype(jnp.int32)
    virt = lax.axis_index("virt").astype(jnp.int32)
    (even,) = regroup(0, me[None], integrals)
    own, plus, far, minus = regroup(1, me[None], integrals)
    even = lax.all_to_all(even, "pair", 0, 0, tiled=True)

    amp = [jnp.transpose(amplitudes[parity], (1, 0, 2)) for parity in range(2)]
    occ_terms = pick(pair_list, eps_occ)
    occ = occ_terms[:, :, 0] + occ_terms[:, :, 1]
    eps_a = eps_virt[:, None]
    scalars = (jnp.stack([me, virt]), virt_counts, pair_counts, eps_virt)

    even, plus, far, minus = lax.optimization_barrier((even, plus, far, minus))
    left, far, right = step(plus, 1), step(far, 2), step(minus, 3)
    send, energy0 = ladder(0, scalars, (even,), amp[0], eps_a, occ)
    first = across(send)
    (send,) = ladder(1, scalars, (own, left, far, right), amp[1], eps_a, occ, energy0)
    first, send = lax.optimization_barrier((first, send))
    second = across(send)
    (out,) = place(0, first)
    return tuple(place(1, second, out))


def solution(mesh):
    placed = (
        P("pair", None, None, None),
        P(None, None, None, ("virt", "pair")),
        P(),
        P(),
        P("pair", None, None),
        P(),
        P(),
    )
    return jax.shard_map(
        shards,
        mesh=mesh,
        in_specs=placed,
        out_specs=(P("pair", None, "virt"), P("pair", "virt")),
        check_vma=False,
    )
```

```python
import jax
import jax.numpy as jnp
from jax import lax
from jax.experimental import pallas as pl
from jax.experimental.pallas import tpu as pltpu
from jax.sharding import PartitionSpec as P

IRREPS = 8
NV = 512
BLK = 64
SLABS = 2
PCAP = 1024
KQ = 256
KS = 1024
VIRTS = 64
OWN = NV // VIRTS
MINE = PCAP // VIRTS
VMEM = 20 * 1024 * 1024
ABLK = 256
SUB = 32
RBLK = 512
EXTRA = 128


def iota(shape, axis):
    return lax.broadcasted_iota(jnp.int32, shape, axis)


def regroup_kernel(parity, pair_ref, x_hbm, *refs):
    outs, (x, held, loads, stores) = refs[:-4], refs[-4:]
    parts = [(slab, block) for slab in range(SLABS) for block in range(NV // ABLK)]
    fetches = []
    for slab, block in parts:
        at = pl.ds(block * ABLK * IRREPS, ABLK * IRREPS)
        fetch = pltpu.make_async_copy(x_hbm.at[slab, at, :], x.at[slab, at, :], loads.at[slab, block])
        fetch.start()
        fetches.append(fetch)
    rows = SUB * IRREPS
    to, source = iota((rows // 2, rows), 0), iota((rows // 2, rows), 1)
    perm = jnp.where((to & (SUB - 1)) * IRREPS + 2 * (to >> 5) + parity == source, 1.0, 0.0).astype(jnp.bfloat16)
    copies = []
    for fetch, (slab, block) in zip(fetches, parts):
        fetch.wait()
        for sub in range(ABLK // SUB):
            first = block * ABLK + sub * SUB
            moved = jnp.dot(
                perm,
                x[slab, first * IRREPS : first * IRREPS + rows, :],
                preferred_element_type=jnp.float32,
            ).astype(jnp.bfloat16)
            for pair in range(4):
                held[pair, slab, first : first + SUB, :] = moved[pair * SUB : (pair + 1) * SUB]
        if parity == 0:
            at = pl.ds(block * ABLK, ABLK)
            copy = pltpu.make_async_copy(
                held.at[:, slab, at, :], outs[0].at[:, slab, at, :], stores.at[slab * (NV // ABLK) + block]
            )
            copy.start()
            copies.append(copy)
    if parity == 1:
        me = pair_ref[0]
        for shift in range(4):
            copy = pltpu.make_async_copy(held.at[(me + shift) % 4], outs[shift], stores.at[shift])
            copy.start()
            copies.append(copy)
    for copy in copies:
        copy.wait()


def regroup(parity, pair_id, integrals):
    if parity == 0:
        shapes = [pltpu.HBM((4, SLABS, NV, KQ), jnp.bfloat16)]
    else:
        shapes = [pltpu.HBM((SLABS, NV, KQ), jnp.bfloat16)] * 4
    flat = pltpu.with_memory_space_constraint(integrals.reshape(SLABS, NV * IRREPS, KQ), pltpu.HBM)
    return pl.pallas_call(
        lambda *refs: regroup_kernel(parity, *refs),
        in_specs=[pl.BlockSpec(memory_space=pltpu.SMEM), pl.BlockSpec(memory_space=pltpu.HBM)],
        out_specs=[pl.BlockSpec(memory_space=pltpu.HBM)] * len(shapes),
        out_shape=shapes,
        scratch_shapes=[
            pltpu.VMEM((SLABS, NV * IRREPS, KQ), jnp.bfloat16),
            pltpu.VMEM((4, SLABS, NV, KQ), jnp.bfloat16),
            pltpu.SemaphoreType.DMA((SLABS, NV // ABLK)),
            pltpu.SemaphoreType.DMA((SLABS * (NV // ABLK),)),
        ],
        compiler_params=pltpu.CompilerParams(vmem_limit_bytes=VMEM),
        cost_estimate=pl.CostEstimate(flops=1 << 30, bytes_accessed=6 << 20, transcendentals=0),
        name="regroup",
    )(pair_id, flat)


def ladder_kernel(parity, ids, virt_counts, pair_counts, eps, *refs):
    if parity == 0:
        pieces, (amp, eps_a, occ, send, energy_out, held, stage, sems, energy) = refs[:-9], refs[-9:]
    else:
        pieces, (amp, eps_a, occ, energy0, send, held, stage, sems, energy, extra) = refs[:-10], refs[-10:]
    me, virt = ids[0], ids[1]
    h = 2 * me + parity
    mask = jnp.where((iota((1, KQ), 1) & (BLK - 1)) < virt_counts[h], 1.0, 0.0).astype(jnp.bfloat16)
    for slab in range(SLABS):
        if parity == 0:
            for source in range(4):
                to = slab * KS + source * KQ
                held[:, to : to + KQ] = pieces[0][source, slab] * mask
        else:
            for shift, piece in zip((0, 3, 2, 1), pieces):
                to = pl.multiple_of(slab * KS + ((me + shift) % 4) * KQ, KQ)
                held[:, pl.ds(to, KQ)] = piece[slab] * mask
    slot = iota((BLK, RBLK), 0)
    column = iota((BLK, RBLK), 1)
    copies = []
    for block in range(PCAP // RBLK):
        at = slice(block * RBLK, (block + 1) * RBLK)
        total = None
        for slab in range(SLABS):
            term = lax.dot_general(
                held[:, slab * KS : (slab + 1) * KS],
                amp[slab, at, :],
                (((1,), (1,)), ((), ())),
                preferred_element_type=jnp.float32,
            )
            total = term if total is None else total + term
        occ_row = occ[parity : parity + 1, at]
        live_row = block * RBLK + column < pair_counts[h]
        summed = jnp.zeros((1, RBLK), jnp.float32)
        for ha in range(IRREPS):
            rows = slice(ha * BLK, (ha + 1) * BLK)
            hb = jnp.bitwise_xor(h, ha)
            part = total[rows]
            denom = (eps_a[rows, :] + eps[hb * BLK + virt]) - occ_row
            live_a = jnp.where(virt < virt_counts[hb], virt_counts[ha], 0)
            ratio = jnp.where((slot < live_a) & live_row, part / denom, 0.0)
            summed = summed + jnp.sum(ratio * part, axis=0, keepdims=True)
            stage[block, rows, :] = ratio.astype(jnp.bfloat16)
        energy[:, at] = summed / (NV * BLK)
        copy = pltpu.make_async_copy(stage.at[block], send.at[:, pl.ds(block * RBLK, RBLK)], sems.at[block])
        copy.start()
        copies.append(copy)
    if parity == 0:
        copy = pltpu.make_async_copy(energy, energy_out, sems.at[PCAP // RBLK])
        copy.start()
        copies.append(copy)
    else:
        value = jnp.concatenate([energy0[...], energy[...]], axis=0)
        high = value.astype(jnp.bfloat16).astype(jnp.float32)
        rest = value - high
        middle = rest.astype(jnp.bfloat16).astype(jnp.float32)
        low = rest - middle
        terms = jnp.concatenate([high, middle, low, jnp.zeros((2, PCAP), jnp.float32)], axis=0)
        spread = jnp.broadcast_to(terms[None], (VIRTS, OWN, PCAP)).reshape(NV, PCAP)
        owner = (iota((NV, PCAP), 1) // MINE) == (iota((NV, PCAP), 0) // OWN)
        spread = jnp.where(owner, spread, 0.0).astype(jnp.bfloat16)
        lane = (iota((PCAP, EXTRA), 0) & (MINE - 1)) == iota((PCAP, EXTRA), 1)
        select = jnp.where(lane, 1.0, 0.0).astype(jnp.bfloat16)
        extra[...] = jnp.dot(spread, select, preferred_element_type=jnp.float32).astype(jnp.bfloat16)
        copy = pltpu.make_async_copy(extra, send.at[:, pl.ds(PCAP, EXTRA)], sems.at[PCAP // RBLK])
        copy.start()
        copies.append(copy)
    for copy in copies:
        copy.wait()


def ladder(parity, scalars, pieces, amp, eps_a, occ, *energy0):
    vmem = pl.BlockSpec(memory_space=pltpu.VMEM)
    columns = PCAP if parity == 0 else PCAP + EXTRA
    row = pltpu.HBM((1, PCAP), jnp.float32)
    scratch = [
        pltpu.VMEM((NV, SLABS * KS), jnp.bfloat16),
        pltpu.VMEM((PCAP // RBLK, NV, RBLK), jnp.bfloat16),
        pltpu.SemaphoreType.DMA((PCAP // RBLK + 1,)),
        pltpu.VMEM((1, PCAP), jnp.float32),
    ]
    if parity == 1:
        scratch.append(pltpu.VMEM((NV, EXTRA), jnp.bfloat16))
    return pl.pallas_call(
        lambda *refs: ladder_kernel(parity, *refs),
        in_specs=[pl.BlockSpec(memory_space=pltpu.SMEM)] * 4
        + [vmem] * (len(pieces) + 3 + len(energy0)),
        out_specs=[pl.BlockSpec(memory_space=pltpu.HBM)] * (2 - parity),
        out_shape=[pltpu.HBM((NV, columns), jnp.bfloat16)] + [row] * (1 - parity),
        scratch_shapes=scratch,
        compiler_params=pltpu.CompilerParams(vmem_limit_bytes=VMEM),
        cost_estimate=pl.CostEstimate(
            flops=(1 + parity * 8) * 2 * NV * PCAP * SLABS * KS, bytes_accessed=7 << 20, transcendentals=0
        ),
        name="ladder",
    )(*scalars, *pieces, amp, eps_a, occ, *energy0)


def place_kernel(parity, block, *refs):
    if parity == 0:
        out, stage, sems = refs
    else:
        _, out, energy_out, stage, sems, energy = refs
    source, to = iota((NV, NV), 0), iota((NV, NV), 1)
    perm = jnp.where((source & (OWN - 1)) * BLK + (source >> 3) == to, 1.0, 0.0).astype(jnp.bfloat16)
    copies = []
    if parity == 1:
        values = block[:, PCAP : PCAP + EXTRA].astype(jnp.float32)
        kind = iota((NV, EXTRA), 0) & (OWN - 1)
        for which in range(2):
            mine = (kind < 6) & ((kind & 1) == which)
            summed = jnp.sum(jnp.where(mine, values, 0.0), axis=0, keepdims=True)
            energy[which : which + 1, :] = summed[:, :MINE]
        copy = pltpu.make_async_copy(energy, energy_out, sems.at[PCAP // RBLK])
        copy.start()
        copies.append(copy)
    for part in range(PCAP // RBLK):
        stage[part] = lax.dot_general(
            block[:, part * RBLK : (part + 1) * RBLK],
            perm,
            (((0,), (0,)), ((), ())),
            preferred_element_type=jnp.float32,
        ).astype(jnp.bfloat16)
        copy = pltpu.make_async_copy(stage.at[part], out.at[parity, pl.ds(part * RBLK, RBLK), :], sems.at[part])
        copy.start()
        copies.append(copy)
    for copy in copies:
        copy.wait()


def place(parity, block, *before):
    vmem = pl.BlockSpec(memory_space=pltpu.VMEM)
    hbm = pl.BlockSpec(memory_space=pl.ANY)
    out = jax.ShapeDtypeStruct((2, PCAP, NV), jnp.bfloat16)
    return pl.pallas_call(
        lambda *refs: place_kernel(parity, *refs),
        in_specs=[vmem] + [hbm] * parity,
        out_specs=[hbm] * (1 + parity),
        out_shape=[out] + [jax.ShapeDtypeStruct((2, MINE), jnp.float32)] * parity,
        input_output_aliases={1: 0} if parity else {},
        scratch_shapes=[
            pltpu.VMEM((PCAP // RBLK, RBLK, NV), jnp.bfloat16),
            pltpu.SemaphoreType.DMA((PCAP // RBLK + 1,)),
        ]
        + [pltpu.VMEM((2, MINE), jnp.float32)] * parity,
        compiler_params=pltpu.CompilerParams(vmem_limit_bytes=VMEM),
        cost_estimate=pl.CostEstimate(flops=2 * NV * NV * PCAP, bytes_accessed=2 << 20, transcendentals=0),
        name="place",
    )(block, *before)


def pick(ids, table):
    onehot = ids[..., None] == jnp.arange(table.shape[0], dtype=jnp.int32)
    return jnp.sum(jnp.where(onehot, table, 0), axis=-1)


def step(value, by):
    return lax.ppermute(value, "pair", [(i, (i + by) % 4) for i in range(4)])


def across(value):
    return lax.all_to_all(value, "virt", 0, 0, tiled=True)


def shards(amplitudes, integrals, virt_counts, pair_counts, pair_list, eps_occ, eps_virt):
    me = lax.axis_index("pair").astype(jnp.int32)
    virt = lax.axis_index("virt").astype(jnp.int32)
    (even,) = regroup(0, me[None], integrals)
    own, plus, far, minus = regroup(1, me[None], integrals)
    even = lax.all_to_all(even, "pair", 0, 0, tiled=True)

    amp = [jnp.transpose(amplitudes[parity], (1, 0, 2)) for parity in range(2)]
    occ_terms = pick(pair_list, eps_occ)
    occ = occ_terms[:, :, 0] + occ_terms[:, :, 1]
    eps_a = eps_virt[:, None]
    scalars = (jnp.stack([me, virt]), virt_counts, pair_counts, eps_virt)

    amp[0], plus, far, minus = lax.optimization_barrier((amp[0], plus, far, minus))
    left, far, right = step(plus, 1), step(far, 2), step(minus, 3)
    send, energy0 = ladder(0, scalars, (even,), amp[0], eps_a, occ)
    first = across(send)
    (send,) = ladder(1, scalars, (own, left, far, right), amp[1], eps_a, occ, energy0)
    first, send = lax.optimization_barrier((first, send))
    second = across(send)
    (out,) = place(0, first)
    return tuple(place(1, second, out))


def solution(mesh):
    placed = (
        P("pair", None, None, None),
        P(None, None, None, ("virt", "pair")),
        P(),
        P(),
        P("pair", None, None),
        P(),
        P(),
    )
    return jax.shard_map(
        shards,
        mesh=mesh,
        in_specs=placed,
        out_specs=(P("pair", None, "virt"), P("pair", "virt")),
        check_vma=False,
    )
```

```python
import jax
import jax.numpy as jnp
from jax import lax
from jax.experimental import pallas as pl
from jax.experimental.pallas import tpu as pltpu
from jax.sharding import PartitionSpec as P

IRREPS = 8
NV = 512
BLK = 64
SLABS = 2
PCAP = 1024
KQ = 256
KS = 1024
VIRTS = 64
OWN = NV // VIRTS
MINE = PCAP // VIRTS
VMEM = 20 * 1024 * 1024
ABLK = 256
SUB = 32
RBLK = 512
EXTRA = 128


def iota(shape, axis):
    return lax.broadcasted_iota(jnp.int32, shape, axis)


def regroup_kernel(parity, pair_ref, x_hbm, *refs):
    outs, (x, held, loads, stores) = refs[:-4], refs[-4:]
    parts = [(slab, block) for slab in range(SLABS) for block in range(NV // ABLK)]
    fetches = []
    for slab, block in parts:
        at = pl.ds(block * ABLK * IRREPS, ABLK * IRREPS)
        fetch = pltpu.make_async_copy(x_hbm.at[slab, at, :], x.at[slab, at, :], loads.at[slab, block])
        fetch.start()
        fetches.append(fetch)
    rows = SUB * IRREPS
    to, source = iota((rows // 2, rows), 0), iota((rows // 2, rows), 1)
    perm = jnp.where((to & (SUB - 1)) * IRREPS + 2 * (to >> 5) + parity == source, 1.0, 0.0).astype(jnp.bfloat16)
    copies = []
    for fetch, (slab, block) in zip(fetches, parts):
        fetch.wait()
        for sub in range(ABLK // SUB):
            first = block * ABLK + sub * SUB
            moved = jnp.dot(
                perm,
                x[slab, first * IRREPS : first * IRREPS + rows, :],
                preferred_element_type=jnp.float32,
            ).astype(jnp.bfloat16)
            for pair in range(4):
                held[pair, slab, first : first + SUB, :] = moved[pair * SUB : (pair + 1) * SUB]
        if parity == 0:
            at = pl.ds(block * ABLK, ABLK)
            copy = pltpu.make_async_copy(
                held.at[:, slab, at, :], outs[0].at[:, slab, at, :], stores.at[slab * (NV // ABLK) + block]
            )
            copy.start()
            copies.append(copy)
    if parity == 1:
        me = pair_ref[0]
        for shift in range(4):
            copy = pltpu.make_async_copy(held.at[(me + shift) % 4], outs[shift], stores.at[shift])
            copy.start()
            copies.append(copy)
    for copy in copies:
        copy.wait()


def regroup(parity, pair_id, integrals):
    if parity == 0:
        shapes = [pltpu.HBM((4, SLABS, NV, KQ), jnp.bfloat16)]
    else:
        shapes = [pltpu.HBM((SLABS, NV, KQ), jnp.bfloat16)] * 4
    flat = pltpu.with_memory_space_constraint(integrals.reshape(SLABS, NV * IRREPS, KQ), pltpu.HBM)
    return pl.pallas_call(
        lambda *refs: regroup_kernel(parity, *refs),
        in_specs=[pl.BlockSpec(memory_space=pltpu.SMEM), pl.BlockSpec(memory_space=pltpu.HBM)],
        out_specs=[pl.BlockSpec(memory_space=pltpu.HBM)] * len(shapes),
        out_shape=shapes,
        scratch_shapes=[
            pltpu.VMEM((SLABS, NV * IRREPS, KQ), jnp.bfloat16),
            pltpu.VMEM((4, SLABS, NV, KQ), jnp.bfloat16),
            pltpu.SemaphoreType.DMA((SLABS, NV // ABLK)),
            pltpu.SemaphoreType.DMA((SLABS * (NV // ABLK),)),
        ],
        compiler_params=pltpu.CompilerParams(vmem_limit_bytes=VMEM),
        cost_estimate=pl.CostEstimate(flops=1 << 30, bytes_accessed=6 << 20, transcendentals=0),
        name="regroup",
    )(pair_id, flat)


def ladder_kernel(parity, ids, virt_counts, pair_counts, eps, *refs):
    if parity == 0:
        pieces, (amp, eps_a, occ, send, energy_out, held, stage, sems, energy) = refs[:-9], refs[-9:]
    else:
        pieces, (amp, eps_a, occ, energy0, send, held, stage, sems, energy, extra) = refs[:-10], refs[-10:]
    me, virt = ids[0], ids[1]
    h = 2 * me + parity
    mask = jnp.where((iota((1, KQ), 1) & (BLK - 1)) < virt_counts[h], 1.0, 0.0).astype(jnp.bfloat16)
    for slab in range(SLABS):
        if parity == 0:
            for source in range(4):
                to = slab * KS + source * KQ
                held[:, to : to + KQ] = pieces[0][source, slab] * mask
        else:
            for shift, piece in zip((0, 3, 2, 1), pieces):
                to = pl.multiple_of(slab * KS + ((me + shift) % 4) * KQ, KQ)
                held[:, pl.ds(to, KQ)] = piece[slab] * mask
    slot = iota((BLK, RBLK), 0)
    column = iota((BLK, RBLK), 1)
    copies = []
    for block in range(PCAP // RBLK):
        at = slice(block * RBLK, (block + 1) * RBLK)
        total = None
        for slab in range(SLABS):
            term = lax.dot_general(
                held[:, slab * KS : (slab + 1) * KS],
                amp[slab, at, :],
                (((1,), (1,)), ((), ())),
                preferred_element_type=jnp.float32,
            )
            total = term if total is None else total + term
        occ_row = occ[parity : parity + 1, at]
        live_row = block * RBLK + column < pair_counts[h]
        summed = jnp.zeros((1, RBLK), jnp.float32)
        for ha in range(IRREPS):
            rows = slice(ha * BLK, (ha + 1) * BLK)
            hb = jnp.bitwise_xor(h, ha)
            part = total[rows]
            denom = (eps_a[rows, :] + eps[hb * BLK + virt]) - occ_row
            live_a = jnp.where(virt < virt_counts[hb], virt_counts[ha], 0)
            ratio = jnp.where((slot < live_a) & live_row, part / denom, 0.0)
            summed = summed + jnp.sum(ratio * part, axis=0, keepdims=True)
            stage[block, rows, :] = ratio.astype(jnp.bfloat16)
        energy[:, at] = summed / (NV * BLK)
        copy = pltpu.make_async_copy(stage.at[block], send.at[:, pl.ds(block * RBLK, RBLK)], sems.at[block])
        copy.start()
        copies.append(copy)
    if parity == 0:
        copy = pltpu.make_async_copy(energy, energy_out, sems.at[PCAP // RBLK])
        copy.start()
        copies.append(copy)
    else:
        value = jnp.concatenate([energy0[...], energy[...]], axis=0)
        high = value.astype(jnp.bfloat16).astype(jnp.float32)
        rest = value - high
        middle = rest.astype(jnp.bfloat16).astype(jnp.float32)
        low = rest - middle
        terms = jnp.concatenate([high, middle, low, jnp.zeros((2, PCAP), jnp.float32)], axis=0)
        spread = jnp.broadcast_to(terms[None], (VIRTS, OWN, PCAP)).reshape(NV, PCAP)
        owner = (iota((NV, PCAP), 1) // MINE) == (iota((NV, PCAP), 0) // OWN)
        spread = jnp.where(owner, spread, 0.0).astype(jnp.bfloat16)
        lane = (iota((PCAP, EXTRA), 0) & (MINE - 1)) == iota((PCAP, EXTRA), 1)
        select = jnp.where(lane, 1.0, 0.0).astype(jnp.bfloat16)
        extra[...] = jnp.dot(spread, select, preferred_element_type=jnp.float32).astype(jnp.bfloat16)
        copy = pltpu.make_async_copy(extra, send.at[:, pl.ds(PCAP, EXTRA)], sems.at[PCAP // RBLK])
        copy.start()
        copies.append(copy)
    for copy in copies:
        copy.wait()


def ladder(parity, scalars, pieces, amp, eps_a, occ, *energy0):
    vmem = pl.BlockSpec(memory_space=pltpu.VMEM)
    columns = PCAP if parity == 0 else PCAP + EXTRA
    row = pltpu.HBM((1, PCAP), jnp.float32)
    scratch = [
        pltpu.VMEM((NV, SLABS * KS), jnp.bfloat16),
        pltpu.VMEM((PCAP // RBLK, NV, RBLK), jnp.bfloat16),
        pltpu.SemaphoreType.DMA((PCAP // RBLK + 1,)),
        pltpu.VMEM((1, PCAP), jnp.float32),
    ]
    if parity == 1:
        scratch.append(pltpu.VMEM((NV, EXTRA), jnp.bfloat16))
    return pl.pallas_call(
        lambda *refs: ladder_kernel(parity, *refs),
        in_specs=[pl.BlockSpec(memory_space=pltpu.SMEM)] * 4
        + [vmem] * (len(pieces) + 3 + len(energy0)),
        out_specs=[pl.BlockSpec(memory_space=pltpu.HBM)] * (2 - parity),
        out_shape=[pltpu.HBM((NV, columns), jnp.bfloat16)] + [row] * (1 - parity),
        scratch_shapes=scratch,
        compiler_params=pltpu.CompilerParams(vmem_limit_bytes=VMEM),
        cost_estimate=pl.CostEstimate(
            flops=(1 + parity * 8) * 2 * NV * PCAP * SLABS * KS, bytes_accessed=7 << 20, transcendentals=0
        ),
        name="ladder",
    )(*scalars, *pieces, amp, eps_a, occ, *energy0)


def place_kernel(parity, block, *refs):
    if parity == 0:
        out, stage, sems = refs
    else:
        _, out, energy_out, stage, sems, energy = refs
    source, to = iota((NV, NV), 0), iota((NV, NV), 1)
    perm = jnp.where((source & (OWN - 1)) * BLK + (source >> 3) == to, 1.0, 0.0).astype(jnp.bfloat16)
    copies = []
    if parity == 1:
        values = block[:, PCAP : PCAP + EXTRA].astype(jnp.float32)
        kind = iota((NV, EXTRA), 0) & (OWN - 1)
        for which in range(2):
            mine = (kind < 6) & ((kind & 1) == which)
            summed = jnp.sum(jnp.where(mine, values, 0.0), axis=0, keepdims=True)
            energy[which : which + 1, :] = summed[:, :MINE]
        copy = pltpu.make_async_copy(energy, energy_out, sems.at[PCAP // RBLK])
        copy.start()
        copies.append(copy)
    for part in range(PCAP // RBLK):
        stage[part] = lax.dot_general(
            block[:, part * RBLK : (part + 1) * RBLK],
            perm,
            (((0,), (0,)), ((), ())),
            preferred_element_type=jnp.float32,
        ).astype(jnp.bfloat16)
        copy = pltpu.make_async_copy(stage.at[part], out.at[parity, pl.ds(part * RBLK, RBLK), :], sems.at[part])
        copy.start()
        copies.append(copy)
    for copy in copies:
        copy.wait()


def place(parity, block, *before):
    vmem = pl.BlockSpec(memory_space=pltpu.VMEM)
    hbm = pl.BlockSpec(memory_space=pl.ANY)
    out = jax.ShapeDtypeStruct((2, PCAP, NV), jnp.bfloat16)
    return pl.pallas_call(
        lambda *refs: place_kernel(parity, *refs),
        in_specs=[vmem] + [hbm] * parity,
        out_specs=[hbm] * (1 + parity),
        out_shape=[out] + [jax.ShapeDtypeStruct((2, MINE), jnp.float32)] * parity,
        input_output_aliases={1: 0} if parity else {},
        scratch_shapes=[
            pltpu.VMEM((PCAP // RBLK, RBLK, NV), jnp.bfloat16),
            pltpu.SemaphoreType.DMA((PCAP // RBLK + 1,)),
        ]
        + [pltpu.VMEM((2, MINE), jnp.float32)] * parity,
        compiler_params=pltpu.CompilerParams(vmem_limit_bytes=VMEM),
        cost_estimate=pl.CostEstimate(flops=2 * NV * NV * PCAP, bytes_accessed=2 << 20, transcendentals=0),
        name="place",
    )(block, *before)


def pick(ids, table):
    onehot = ids[..., None] == jnp.arange(table.shape[0], dtype=jnp.int32)
    return jnp.sum(jnp.where(onehot, table, 0), axis=-1)


def step(value, by):
    return lax.ppermute(value, "pair", [(i, (i + by) % 4) for i in range(4)])


def across(value):
    return lax.all_to_all(value, "virt", 0, 0, tiled=True)


def shards(amplitudes, integrals, virt_counts, pair_counts, pair_list, eps_occ, eps_virt):
    me = lax.axis_index("pair").astype(jnp.int32)
    virt = lax.axis_index("virt").astype(jnp.int32)
    (even,) = regroup(0, me[None], integrals)
    own, plus, far, minus = regroup(1, me[None], integrals)
    even = lax.all_to_all(even, "pair", 0, 0, tiled=True)

    amp = [jnp.transpose(amplitudes[parity], (1, 0, 2)) for parity in range(2)]
    occ_terms = pick(pair_list, eps_occ)
    occ = occ_terms[:, :, 0] + occ_terms[:, :, 1]
    eps_a = eps_virt[:, None]
    scalars = (jnp.stack([me, virt]), virt_counts, pair_counts, eps_virt)

    amp[0], far = lax.optimization_barrier((amp[0], far))
    occ, plus, minus = lax.optimization_barrier((occ, plus, minus))
    left, far, right = step(plus, 1), step(far, 2), step(minus, 3)
    send, energy0 = ladder(0, scalars, (even,), amp[0], eps_a, occ)
    first = across(send)
    (send,) = ladder(1, scalars, (own, left, far, right), amp[1], eps_a, occ, energy0)
    first, send = lax.optimization_barrier((first, send))
    second = across(send)
    (out,) = place(0, first)
    return tuple(place(1, second, out))


def solution(mesh):
    placed = (
        P("pair", None, None, None),
        P(None, None, None, ("virt", "pair")),
        P(),
        P(),
        P("pair", None, None),
        P(),
        P(),
    )
    return jax.shard_map(
        shards,
        mesh=mesh,
        in_specs=placed,
        out_specs=(P("pair", None, "virt"), P("pair", "virt")),
        check_vma=False,
    )
```
